128 devices in a mesh: grid: 4 (over x), blk: 32 (over z, y, core).
Axes of the slice: x: 4, y: 4, z: 4, core: 2. Of those that a mesh axis runs over, the one named last changes fastest.
Arguments:
- state: float32 [4, 4, 128, 128, 128], P('grid', None, 'blk'), may hold values from -6 to 6
- metric: float32 [4, 9, 128, 128, 128], P('grid', None, 'blk'), may hold values from -3 to 3
- damping: float32 [4, 128, 128, 128], P('grid', 'blk'), may hold values from 0 to 1.5
- donor: int32 [4, 131072], P('grid', 'blk'), may hold values from 16384 to 81790, as said below
- fractions: float32 [4, 3, 131072], P('grid', None, 'blk'), may hold values from 0 to 1
- dest: int32 [4, 131072, 1], P('grid', 'blk'), may hold values from 0 to 127; in each aligned block of 4096 rows (0 to 4095, 4096 to 8191, ..., all dimensions but the last counted through in order) at most 64 rows name the same one
- recept: int32 [4, 131072], P('grid', 'blk'), may hold values from 0 to 65535
Outputs:
- updated: float32 [4, 4, 128, 128, 128], P('grid', None, 'blk')
The draws below stay inside these ranges and needn't reach their ends.
Inputs may be any that keep to these rules, and one draw needn't show every extreme that they name: A flat index a * 128 * 128 + c * 128 + e into the donor's block extended by one cell at both ends of the first dimension, with a from 1 to 4 (to 3 on the last block of each grid), c below 127 and e below 127. `dest`: among the rows of one device, at most 64 name the same receiving block. `recept`: a cell of the receiving block, flat over its three dimensions.
All inputs are finite; a program needn't handle non-finite values.
Results may differ from the reference program's by a relative error of at most 0.00002.
Values sent between devices are 32-bit elements; how exact they have to be, the bound alone decides.
No kernel may reach another device: no remote copies, remote signals or barrier semaphores. Data moves between devices by JAX's collectives and lax.ppermute only.
A program may use at most 192 MiB of HBM per device.

```python
import math
import jax
import jax.numpy as jnp
import numpy as np

CX = 4
CY = 128
CZ = 128
DONORS = 4096
GRIDS = 4
BLOCKS = 32
NX = 128
ROWS = 131072
CAP = 64


def draw_donor(key, part):
    key = jax.random.fold_in(key, 11)
    key_x, key_y, key_z = jax.random.split(key, 3)
    row_index = jnp.arange(ROWS, dtype=jnp.int32)
    last_block = row_index // DONORS == ROWS // DONORS - 1
    upper_x = jnp.where(last_block, CX, CX + 1)
    shape_all = (GRIDS, ROWS)
    index_x = jax.random.randint(key_x, shape_all, 1, upper_x[None, :])
    index_y = jax.random.randint(key_y, shape_all, 0, CY - 1)
    index_z = jax.random.randint(key_z, shape_all, 0, CZ - 1)
    flattened = index_x * (CY * CZ) + index_y * CZ + index_z
    highest = CX * CY * CZ + (CY - 2) * CZ + CZ - 2
    lowest = CY * CZ
    grid_index = jnp.arange(GRIDS, dtype=jnp.int32)[:, None]
    first_row = (grid_index == 0) & (row_index[None, :] == 0)
    second_row = (grid_index == 0) & (row_index[None, :] == 1)
    flattened = jnp.where(first_row, highest, flattened)
    flattened = jnp.where(second_row, lowest, flattened)
    return flattened.astype(jnp.int32)


def with_ends(array, stream_key, smallest, top_value):
    index_at = [jax.random.randint(jax.random.fold_in(stream_key, axis), (), 0, length) for axis, length in enumerate(array.shape)]
    main_axis = array.shape.index(max(array.shape))
    neighbour = index_at[:main_axis] + [(index_at[main_axis] + 1) % array.shape[main_axis]] + index_at[main_axis + 1:]
    return array.at[tuple(index_at)].set(smallest).at[tuple(neighbour)].set(top_value)


def level_of(key, dims, cuts, least, largest):
    loudness = 1.0
    for dim, shards_of in cuts:
        draws = jax.random.uniform(jax.random.fold_in(jax.random.fold_in(key, 6), dim), (shards_of,), jnp.float32, least / len(cuts), largest / len(cuts))
        loudness = loudness * jnp.repeat(jnp.exp(draws), dims[dim] // shards_of).reshape((-1,) + (1,) * (len(dims) - 1 - dim))
    return loudness


def deal_out(rng, own, number, rows, number_of, top, bound, skew):
    order = jax.random.permutation(rng, number_of)
    packed, common = shares(number_of, rows * top, bound, skew, True), shares(number_of, rows * top, bound, skew, False)
    places = jnp.arange(number_of)

    def named(lengths, turn):
        used = int((lengths > 0).sum())
        fixed = max(1, used // 4)
        shifted = fixed + (places - fixed + turn * (used - fixed)) % max(1, number_of - fixed)
        return jnp.zeros((number_of,), jnp.int32).at[order[jnp.where(places < fixed, places, shifted)]].set(jnp.asarray(lengths, jnp.int32))

    lengths = jnp.where(number % 4 == 0, named(packed, number // 4), named(common, number - number // 4 - 1))
    mixed = jax.random.permutation(jax.random.fold_in(own, 3), number_of)
    giver, receiver = mixed[0:number_of // 2 * 2:2], mixed[1:number_of // 2 * 2:2]
    room = jnp.minimum(lengths[giver] - 1, bound - lengths[receiver]) // 2
    room = jnp.where((giver == order[0]) | (receiver == order[0]) | (lengths[receiver] == 0), 0, jnp.maximum(room, 0))
    shifted = jax.random.randint(jax.random.fold_in(own, 4), (number_of // 2,), 0, 1 << 20) % (room + 1)
    lengths = lengths.at[giver].add(-shifted).at[receiver].add(shifted)
    items = jnp.searchsorted(jnp.cumsum(lengths), jnp.arange(rows * top), side="right").astype(jnp.int32)
    table = items.reshape(top, rows).T
    table = table[jax.random.permutation(jax.random.fold_in(own, 1), rows)]
    turn = jax.random.randint(jax.random.fold_in(own, 2), (rows, 1), 0, top)
    return jnp.take_along_axis(table, (jnp.arange(top)[None, :] + turn) % top, axis=1)


def shares(amount, total, most, skew, full):
    weights = [(1 << 20) // math.isqrt(standing ** skew) + 1 for standing in range(1, amount + 1)]
    largest = most if full else min(most, max(-(-total // amount), total * weights[0] // sum(weights)))
    least = 1 if total - largest >= amount - 1 else 0
    counts, rest = [largest] + [least] * (amount - 1), total - largest - least * (amount - 1)
    while rest > 0:
        movable = [i for i in range(1, amount) if counts[i] < largest] or [i for i in range(1, amount) if counts[i] < most]
        whole, left = sum([weights[i] for i in movable]), rest
        for i in movable:
            extra = min(most - counts[i], max(1, left * weights[i] // whole), rest)
            counts[i] = counts[i] + extra
            rest = rest - extra
    return np.array(counts)


def centred(key, dims, width, bound, pieces=(), held_as=jnp.bfloat16):
    array = jax.random.normal(key, dims, jnp.float32) * width
    if len(pieces) > 0:
        array = level_of(key, dims, pieces, -0.22, 0.18) * array
    return jnp.clip(array, min=-bound, max=bound).astype(held_as)


def setup_inputs(seed: int = 0) -> dict:
    splits = jax.random.split(jax.random.key(seed), 8)
    state = centred(splits[0], (GRIDS, 4, NX, CY, CZ), 1.0, 6.0, ((0, 4), (2, 32)), jnp.float32)
    metric = centred(splits[1], (GRIDS, 9, NX, CY, CZ), 0.6, 3.0, ((0, 4), (2, 32)), jnp.float32)
    damping = jnp.clip(1.5 * jax.random.uniform(splits[2], (GRIDS, NX, CY, CZ), jnp.float32) ** level_of(splits[2], (GRIDS, NX, CY, CZ), ((0, 4), (1, 32)), -0.2, 0.2), 0.0, 1.5)
    donor = draw_donor(jax.random.fold_in(splits[7], 71), 0)
    fractions = jnp.clip(1.0 * jax.random.uniform(splits[4], (GRIDS, 3, ROWS), jnp.float32) ** level_of(splits[4], (GRIDS, 3, ROWS), ((0, 4), (2, 32)), -0.2, 0.2), 0.0, 1.0)
    dest_keys = jax.random.split(jax.random.fold_in(splits[5], 1), GRIDS * ROWS // DONORS)
    dest_turns = jax.random.permutation(jax.random.fold_in(splits[5], 3), GRIDS * ROWS // DONORS)
    dest = jax.vmap(lambda own, number: deal_out(jax.random.fold_in(splits[5], 2), own, number, DONORS, GRIDS * BLOCKS, 1, CAP, 2))(dest_keys, dest_turns).reshape((GRIDS, ROWS, 1))
    recept = with_ends(jax.random.randint(splits[6], (GRIDS, ROWS), 0, CX * CY * CZ), jax.random.fold_in(splits[6], 1), 0, (CX * CY * CZ) - 1).astype(jnp.int32)
    return {"state": state, "metric": metric, "damping": damping, "donor": donor, "fractions": fractions, "dest": dest, "recept": recept}


step_size = 0.4
penalty = 1.0


def tendency(extended, metric, damping, fringe_sum, fringe_count):
    padded = jnp.pad(extended, ((0, 0), (0, 0), (1, 1), (1, 1)))
    interior = extended[:, 1:-1]
    differences = (
        (padded[:, 2:, 1:-1, 1:-1] - padded[:, :-2, 1:-1, 1:-1]) * 0.5,
        (padded[:, 1:-1, 2:, 1:-1] - padded[:, 1:-1, :-2, 1:-1]) * 0.5,
        (padded[:, 1:-1, 1:-1, 2:] - padded[:, 1:-1, 1:-1, :-2]) * 0.5,
    )

    def gradient(component, direction):
        return (metric[direction] * differences[0][component]
                + metric[3 + direction] * differences[1][component]
                + metric[6 + direction] * differences[2][component])

    pressure = -(gradient(1, 0) + gradient(2, 1) + gradient(3, 2))
    fluxes = jnp.stack([pressure, -gradient(0, 0), -gradient(0, 1), -gradient(0, 2)])
    return fluxes - damping[None] * interior + penalty * (fringe_sum - fringe_count[None] * interior)


def interpolate(extended, base_index, fractions):
    plane_size = extended.shape[2] * extended.shape[3]
    line_size = extended.shape[3]
    flattened = extended.reshape(extended.shape[0], -1)
    accumulated = jnp.zeros((extended.shape[0], base_index.shape[0]), jnp.float32)
    for shift_x in (0, 1):
        weight_x = fractions[0] if shift_x else 1.0 - fractions[0]
        for shift_y in (0, 1):
            weight_y = fractions[1] if shift_y else 1.0 - fractions[1]
            for shift_z in (0, 1):
                weight_z = fractions[2] if shift_z else 1.0 - fractions[2]
                offset = shift_x * plane_size + shift_y * line_size + shift_z
                corner = jnp.take(flattened, base_index + offset, axis=1)
                accumulated = accumulated + (weight_x * weight_y * weight_z)[None] * corner
    return accumulated


def reference(state, metric, damping, donor, fractions, dest, recept):
    cell_count = CX * CY * CZ
    device_count = GRIDS * BLOCKS
    target = (dest[:, :, 0] * cell_count + recept).reshape(-1)
    row_index = jnp.arange(ROWS, dtype=jnp.int32)
    base_index = donor + ((row_index // DONORS) * cell_count)[None, :]
    arrivals = jnp.zeros((device_count * cell_count,), jnp.float32).at[target].add(1.0)
    arrivals = arrivals.reshape(GRIDS, NX, CY, CZ)

    def rates(current):
        extended = jnp.pad(current, ((0, 0), (0, 0), (1, 1), (0, 0), (0, 0)))
        values = jax.vmap(interpolate)(extended, base_index, fractions)
        values = jnp.transpose(values, (1, 0, 2)).reshape(4, -1)
        deposited = jnp.zeros((4, device_count * cell_count), jnp.float32).at[:, target].add(values)
        deposited = jnp.transpose(deposited.reshape(4, GRIDS, NX, CY, CZ), (1, 0, 2, 3, 4))
        return jnp.stack([tendency(extended[grid_number], metric[grid_number], damping[grid_number],
                                   deposited[grid_number], arrivals[grid_number])
                          for grid_number in range(GRIDS)])

    first_rate = rates(state)
    section = state + step_size * first_rate
    second_rate = rates(section)
    return state + 0.5 * step_size * (first_rate + second_rate)
```

```python
import functools
import jax
import jax.numpy as jnp
from jax import lax
from jax.experimental import pallas as pl
from jax.experimental.pallas import tpu as pltpu
from jax.sharding import PartitionSpec as P

step_size = 0.4
f32, bf16, i32 = jnp.float32, jnp.bfloat16, jnp.int32
VMEM_LIMIT = 48 * 1024 * 1024
NT = (((1,), (1,)), ((), ()))


def iota(shape, dim):
    return lax.broadcasted_iota(i32, shape, dim)


def two_parts(x):
    high = x.astype(bf16)
    low = (x - high.astype(f32)).astype(bf16)
    return high, low


def params():
    return pltpu.CompilerParams(vmem_limit_bytes=VMEM_LIMIT)


def pack_kernel(with_labels, state, beyond, donor, fractions, dest, *rest):
    if with_labels:
        recept, out, ranks, source, total = rest
    else:
        ranks, out, source, total = rest
    tile = 256
    tiles = donor.shape[1] // tile
    for c in range(4):
        for x in range(5):
            block = state[c, x] if x < 4 else beyond[c]
            high, low = two_parts(block)
            rows = slice(c * 128, c * 128 + 128)
            source[rows, x * 128 : x * 128 + 128] = high
            source[rows, 640 + x * 128 : 640 + x * 128 + 128] = low
            source[rows, 1280 + x * 128 : 1280 + x * 128 + 128] = high
    total[...] = jnp.zeros_like(total)
    blocks = iota((128, tile), 0)
    cells = iota((128, tile), 0)
    slots = iota((64, tile), 0)
    before = (iota((tile, tile), 0) < iota((tile, tile), 1)).astype(f32).astype(bf16)

    def step(t, counted):
        here = pl.ds(pl.multiple_of(t * tile, tile), tile)
        member = blocks == dest[:, here]
        member_f = member.astype(f32)
        member_b = member_f.astype(bf16)
        if with_labels:
            earlier = jnp.dot(member_b, before, preferred_element_type=f32) + counted
            rank = jnp.sum(member_f * earlier, axis=0, keepdims=True).astype(i32)
            ranks[:, here] = rank
            counted = counted + jnp.sum(member_f, axis=1, keepdims=True)
        else:
            rank = ranks[:, here]
        base = donor[:, here]
        plane = base >> 14
        line = (base >> 7) & 127
        point = base & 127
        fx, fy, fz = fractions[0:1, here], fractions[1:2, here], fractions[2:3, here]
        wy = jnp.where(cells == line, 1.0 - fy, jnp.where(cells == line + 1, fy, 0.0))
        wz = jnp.where(cells == point, 1.0 - fz, jnp.where(cells == point + 1, fz, 0.0))
        highs, lows = [], []
        for x in range(5):
            wx = jnp.where(plane == x + 1, 1.0 - fx, jnp.where(plane == x, fx, 0.0))
            high, low = two_parts(wx * wz)
            highs.append(high)
            lows.append(low)
        weights = jnp.concatenate(highs + highs + lows, axis=0)
        lines = jnp.dot(source[...], weights, preferred_element_type=f32)
        chosen = slots == rank
        parts = []
        values = [
            jnp.sum(lines[c * 128 : c * 128 + 128] * wy, axis=0, keepdims=True) for c in range(4)
        ]
        for which in (0, 1):
            for c in range(4):
                part = two_parts(values[c])[which].astype(f32)
                parts.append(jnp.where(chosen, part, 0.0).astype(bf16))
        if with_labels:
            label = recept[:, here] + 1
            for part in (label >> 8, label & 255):
                parts.append(jnp.where(chosen, part.astype(f32), 0.0).astype(bf16))
        packed = jnp.concatenate(parts, axis=0)
        total[...] += lax.dot_general(member_b, packed, NT, preferred_element_type=f32)
        return counted

    lax.fori_loop(0, tiles, step, jnp.zeros((128, 1), f32))
    for half in range(2):
        cut = slice(half * 128, half * 128 + 128)
        low = slice(256 + half * 128, 256 + half * 128 + 128)
        out[:, half, :] = total[:, cut] + total[:, low]
    if with_labels:
        labels = total[:, 512:640]
        lane = iota((128, 128), 1)
        labels = labels * jnp.where(lane < 64, 256.0, 1.0)
        out[:, 2, :] = labels + pltpu.roll(labels, 64, 1)
        out[:, 3, :] = jnp.zeros((128, 128), f32)


def pack(state, beyond, donor, fractions, dest, recept=None, ranks=None):
    rows = donor.shape[1]
    first = ranks is None
    out = jax.ShapeDtypeStruct((128, 4 if first else 2, 128), f32)
    scratch = [pltpu.VMEM((512, 1920), bf16), pltpu.VMEM((128, 640 if first else 512), f32)]
    if first:
        return pl.pallas_call(
            functools.partial(pack_kernel, True),
            out_shape=(out, jax.ShapeDtypeStruct((1, rows), i32)),
            scratch_shapes=scratch,
            compiler_params=params(),
        )(state, beyond, donor, fractions, dest, recept)
    return pl.pallas_call(
        functools.partial(pack_kernel, False),
        out_shape=out,
        scratch_shapes=scratch,
        compiler_params=params(),
    )(state, beyond, donor, fractions, dest, ranks)


def flux_kernel(state, below, beyond, metric, damping, out):
    row = iota((128, 128), 0)
    lane = iota((128, 128), 1)

    def step(x, _):
        def differences(c):
            here = state[c, x]
            low = jnp.where(x == 0, below[c], state[c, jnp.maximum(x - 1, 0)])
            high = jnp.where(x == 3, beyond[c], state[c, jnp.minimum(x + 1, 3)])
            up = jnp.where(row < 127, pltpu.roll(here, 127, 0), 0.0)
            down = jnp.where(row > 0, pltpu.roll(here, 1, 0), 0.0)
            right = jnp.where(lane < 127, pltpu.roll(here, 127, 1), 0.0)
            left = jnp.where(lane > 0, pltpu.roll(here, 1, 1), 0.0)
            return (high - low) * 0.5, (up - down) * 0.5, (right - left) * 0.5

        def gradient(diffs, i):
            return metric[i, x] * diffs[0] + metric[3 + i, x] * diffs[1] + metric[6 + i, x] * diffs[2]

        damp = damping[x]
        diffs = differences(0)
        for i in range(3):
            out[1 + i, x] = -gradient(diffs, i) - damp * state[1 + i, x]
        pressure = -damp * state[0, x]
        for i in range(3):
            pressure = pressure - gradient(differences(1 + i), i)
        out[0, x] = pressure
        return 0

    lax.fori_loop(0, 4, step, 0)


def flux(state, below, beyond, metric, damping):
    return pl.pallas_call(
        flux_kernel,
        out_shape=jax.ShapeDtypeStruct(state.shape, f32),
        compiler_params=params(),
        cost_estimate=pl.CostEstimate(
            flops=65536 * 80, bytes_accessed=5 * 1024 * 1024, transcendentals=0
        ),
    )(state, below, beyond, metric, damping)


def deposit_kernel(with_labels, *refs):
    if with_labels:
        arrived, now, rates, labels, counts, section, base, slots, total = refs
    else:
        arrived, now, rates, labels, counts, base, out, slots, total = refs
    lane = iota((64, 128), 1)

    def halves(j):
        first, second = arrived[0:64, j, :], arrived[64:128, j, :]
        return (
            jnp.where(lane < 64, first, pltpu.roll(second, 64, 1)),
            jnp.where(lane < 64, pltpu.roll(first, 64, 1), second),
        )

    values = halves(0) + halves(1)
    for c in range(4):
        high = values[c].astype(bf16).astype(f32)
        slots[c] = high
        slots[4 + c] = values[c] - high
    if with_labels:
        labels[...] = halves(2)[0].astype(i32) - 1
    total[...] = jnp.zeros_like(total)
    lines = iota((512, 128), 0)
    points = iota((128, 128), 0)
    chunk = 8

    def step(t, _):
        selectors, spreads = [], []
        for j in range(chunk):
            label = labels[pl.ds(t * chunk + j, 1), :]
            selectors.append((lines == (label >> 7)).astype(f32).astype(bf16))
            at = points == (label & 127)
            column = [
                jnp.where(at, slots[p, pl.ds(t * chunk + j, 1), :], 0.0).astype(bf16)
                for p in range(8)
            ]
            if with_labels:
                column.append(at.astype(f32).astype(bf16))
            spreads.append(jnp.concatenate(column, axis=0))
        selector = jnp.concatenate(selectors, axis=1)
        spread = jnp.concatenate(spreads, axis=1)
        total[...] += lax.dot_general(selector, spread, NT, preferred_element_type=f32)
        return 0

    lax.fori_loop(0, 64 // chunk, step, 0)
    for x in range(4):
        rows = slice(x * 128, x * 128 + 128)
        if with_labels:
            counts[x] = total[rows, 1024:1152]
        for c in range(4):
            fringe = total[rows, c * 128 : c * 128 + 128] + total[rows, 512 + c * 128 : 640 + c * 128]
            rate = rates[c, x] + fringe - counts[x] * now[c, x]
            if with_labels:
                section[c, x] = now[c, x] + step_size * rate
                base[c, x] = now[c, x] + (0.5 * step_size) * rate
            else:
                out[c, x] = base[c, x] + (0.5 * step_size) * rate


def deposit_first(arrived, state, rates):
    return pl.pallas_call(
        functools.partial(deposit_kernel, True),
        out_shape=(
            jax.ShapeDtypeStruct((64, 128), i32),
            jax.ShapeDtypeStruct(state.shape[1:], f32),
            jax.ShapeDtypeStruct(state.shape, f32),
            jax.ShapeDtypeStruct(state.shape, f32),
        ),
        scratch_shapes=[pltpu.VMEM((8, 64, 128), f32), pltpu.VMEM((512, 1152), f32)],
        compiler_params=params(),
    )(arrived, state, rates)


def deposit_second(arrived, section, rates, labels, counts, base):
    return pl.pallas_call(
        functools.partial(deposit_kernel, False),
        out_shape=jax.ShapeDtypeStruct(section.shape, f32),
        scratch_shapes=[pltpu.VMEM((8, 64, 128), f32), pltpu.VMEM((512, 1024), f32)],
        compiler_params=params(),
    )(arrived, section, rates, labels, counts, base)


def neighbours(values):
    count = lax.axis_size("blk")
    forward = [(i, i + 1) for i in range(count - 1)]
    backward = [(i + 1, i) for i in range(count - 1)]
    beyond = lax.ppermute(values[:, 0], "blk", backward)
    below = lax.ppermute(values[:, 3], "blk", forward)
    return below, beyond


def exchange(outgoing):
    return lax.all_to_all(outgoing, ("grid", "blk"), split_axis=0, concat_axis=0, tiled=True)


def local(state, metric, damping, donor, fractions, dest, recept):
    state, metric, damping, fractions = state[0], metric[0], damping[0], fractions[0]
    dest = dest.reshape(1, -1)
    below, beyond = neighbours(state)
    outgoing, ranks = pack(state, beyond, donor, fractions, dest, recept=recept)
    arrived = exchange(outgoing)
    rates = flux(state, below, beyond, metric, damping)
    labels, counts, section, base = deposit_first(arrived, state, rates)
    below, beyond = neighbours(section)
    arrived = exchange(pack(section, beyond, donor, fractions, dest, ranks=ranks))
    rates = flux(section, below, beyond, metric, damping)
    return deposit_second(arrived, section, rates, labels, counts, base)[None]


def solution(mesh):
    in_specs = (
        P("grid", None, "blk", None, None),
        P("grid", None, "blk", None, None),
        P("grid", "blk", None, None),
        P("grid", "blk"),
        P("grid", None, "blk"),
        P("grid", "blk", None),
        P("grid", "blk"),
    )
    out_specs = P("grid", None, "blk", None, None)
    return jax.shard_map(local, mesh=mesh, in_specs=in_specs, out_specs=out_specs, check_vma=False)
```

```python
import functools
import jax
import jax.numpy as jnp
from jax import lax
from jax.experimental import pallas as pl
from jax.experimental.pallas import tpu as pltpu
from jax.sharding import PartitionSpec as P

step_size = 0.4
f32, bf16, i32 = jnp.float32, jnp.bfloat16, jnp.int32
VMEM_LIMIT = 40 * 1024 * 1024
NT = (((1,), (1,)), ((), ()))


def iota(shape, dim):
    return lax.broadcasted_iota(i32, shape, dim)


def two_parts(x):
    high = x.astype(bf16)
    low = (x - high.astype(f32)).astype(bf16)
    return high, low


def params():
    return pltpu.CompilerParams(vmem_limit_bytes=VMEM_LIMIT)


TILE = 256
GROUP = 4
DONOR_ROWS = 24
ARRIVAL_ROWS = 40


def placed(kinds):
    spaces = {"v": pltpu.VMEM, "s": pltpu.SMEM, "h": pltpu.HBM}
    return [pl.BlockSpec(memory_space=spaces[kind]) for kind in kinds]


def exact(mask):
    return mask.astype(f32).astype(bf16)


def starts_of(counts):
    tiles = [(count + TILE - 1) // TILE for count in counts]
    first = tiles[0]
    second = first + tiles[1]
    third = second + tiles[2]
    return first, second, third, third + tiles[3]


def bucket_of(t, starts):
    return sum((t >= starts[i]).astype(i32) for i in range(3))


def prepare_kernel(donor, fractions, dest, recept, table, labels, starts, total):
    width = 512
    rows = donor.shape[1]
    plane_all = donor[...] >> 14
    counts = [jnp.sum((plane_all == p + 1).astype(f32)).astype(i32) for p in range(4)]
    begin = starts_of(counts)
    for i in range(4):
        starts[i] = begin[i]
    offsets = (0,) + begin[:3]
    total[...] = jnp.zeros_like(total)
    labels[...] = jnp.zeros_like(labels)
    blocks = iota((144, width), 0)
    slots = iota((64, width), 0)
    high_rows = iota((DONOR_ROWS, width), 0)
    low_rows = iota((TILE, width), 0)
    before = exact(iota((width, width), 0) < iota((width, width), 1))
    blank = jnp.zeros((8, width), f32)

    def step(t, counted):
        here = pl.ds(pl.multiple_of(t * width, width), width)
        base = donor[:, here]
        plane = base >> 14
        target = dest[:, here]
        member = ((blocks == target) | (blocks == plane + 127)).astype(f32)
        member_b = member.astype(bf16)
        earlier = jnp.dot(member_b, before, preferred_element_type=f32) + counted
        ranked = member * earlier
        rank = jnp.sum(ranked[:128], axis=0, keepdims=True)
        spot = jnp.sum(ranked[128:], axis=0, keepdims=True).astype(i32)
        counted = counted + jnp.sum(member, axis=1, keepdims=True)
        offset = jnp.where(plane == 1, offsets[0], jnp.where(plane == 2, offsets[1], jnp.where(plane == 3, offsets[2], offsets[3])))
        high = offset + (spot >> 8)
        low = spot & 255
        chosen = high_rows == high
        fields = [((base >> 7) & 127).astype(f32), (base & 127).astype(f32), target.astype(f32), rank + 1.0]
        for i in range(3):
            rest = fractions[i, :, here]
            for _ in range(3):
                part = rest.astype(bf16).astype(f32)
                fields.append(part)
                rest = rest - part
        spread = jnp.concatenate([jnp.where(chosen, field, 0.0) for field in fields] + [blank], axis=0)
        total[...] += lax.dot_general(spread.astype(bf16), exact(low_rows == low), NT, preferred_element_type=f32)
        held = slots == rank.astype(i32)
        label = recept[:, here] + 1
        marks = [jnp.where(held, part.astype(f32), 0.0) for part in (label >> 8, label & 255)]
        marks = jnp.concatenate(marks, axis=0).astype(bf16)
        labels[...] += lax.dot_general(member_b[:128], marks, NT, preferred_element_type=f32)
        return counted

    lax.fori_loop(0, rows // width, step, jnp.zeros((144, 1), f32))

    def field(i):
        return total[i * DONOR_ROWS : (i + 1) * DONOR_ROWS]

    for i in range(4):
        table[i] = field(i)
    for i in range(3):
        table[4 + i] = field(4 + 3 * i) + field(5 + 3 * i) + field(6 + 3 * i)
    both = labels[...] * jnp.where(iota((128, 128), 1) < 64, 256.0, 1.0)
    labels[...] = both + pltpu.roll(both, 64, 1)


def prepare(donor, fractions, dest, recept):
    return pl.pallas_call(
        prepare_kernel,
        out_shape=(
            jax.ShapeDtypeStruct((7, DONOR_ROWS, TILE), f32),
            jax.ShapeDtypeStruct((128, 128), f32),
            jax.ShapeDtypeStruct((4,), i32),
        ),
        in_specs=placed("vvvv"),
        out_specs=tuple(placed("vvs")),
        scratch_shapes=[pltpu.VMEM((13 * DONOR_ROWS + 8, TILE), f32)],
        compiler_params=params(),
        cost_estimate=pl.CostEstimate(flops=3 * 10**9, bytes_accessed=10**6, transcendentals=0),
    )(donor, fractions, dest, recept)


def pack_kernel(with_labels, fetched, below, beyond, table, starts, *rest):
    del below
    if with_labels:
        labels, out, source, total, state, sems = rest
    else:
        out, source, total, state, sems = rest
    copies = [pltpu.make_async_copy(fetched.at[c], state.at[c], sems.at[c]) for c in range(4)]
    for copy in copies:
        copy.start()
    for c in range(4):
        copies[c].wait()
        rows = slice(c * 128, c * 128 + 128)
        for x in range(5):
            high, low = two_parts(state[c, x] if x < 4 else beyond[c])
            for pair, side in ((x, 0), (x - 1, 128)):
                if 0 <= pair < 4:
                    for begin, part in ((0, high), (256, low), (512, high)):
                        source[pair, rows, begin + side : begin + side + 128] = part
    total[...] = jnp.zeros_like(total)
    cells = iota((128, TILE), 0)
    slots = iota((64, TILE), 0)
    begin = tuple(starts[i] for i in range(4))

    def interpolated(t):
        line, point, target, rank, fx, fy, fz = (table[i, pl.ds(t, 1), :] for i in range(7))
        line, point, target, rank = (v.astype(i32) for v in (line, point, target, rank))
        wy = jnp.where(cells == line, 1.0 - fy, jnp.where(cells == line + 1, fy, 0.0))
        wz = jnp.where(cells == point, 1.0 - fz, jnp.where(cells == point + 1, fz, 0.0))
        first, second = two_parts(wz * (1.0 - fx)), two_parts(wz * fx)
        high = [first[0], second[0]]
        weights = jnp.concatenate(high + high + [first[1], second[1]], axis=0)
        lines = jnp.dot(source[bucket_of(t, begin)], weights, preferred_element_type=f32)
        chosen = slots == rank - 1
        values = [jnp.sum(lines[c * 128 : c * 128 + 128] * wy, axis=0, keepdims=True) for c in range(4)]
        parts = []
        for which in (0, 1):
            for c in range(4):
                part = two_parts(values[c])[which].astype(f32)
                parts.append(jnp.where(chosen, part, 0.0).astype(bf16))
        return exact(cells == target), jnp.concatenate(parts, axis=0)

    def step(t, _):
        members, packed = zip(*[interpolated(t * GROUP + j) for j in range(GROUP)])
        members, packed = jnp.concatenate(members, axis=1), jnp.concatenate(packed, axis=1)
        total[...] += lax.dot_general(members, packed, NT, preferred_element_type=f32)
        return 0

    lax.fori_loop(0, (begin[3] + GROUP - 1) // GROUP, step, 0)
    for half in range(2):
        cut = slice(half * 128, half * 128 + 128)
        low = slice(256 + half * 128, 256 + half * 128 + 128)
        out[:, half, :] = total[:, cut] + total[:, low]
    if with_labels:
        out[:, 2, :] = labels[...]
        out[:, 3, :] = jnp.zeros((128, 128), f32)


def pack(state, below, beyond, table, starts, labels=None):
    first = labels is not None
    operands = (state, below, beyond, table, starts) + ((labels,) if first else ())
    return pl.pallas_call(
        functools.partial(pack_kernel, first),
        out_shape=jax.ShapeDtypeStruct((128, 4 if first else 2, 128), f32),
        in_specs=placed("hhvvsv"[: len(operands)]),
        out_specs=placed("v")[0],
        scratch_shapes=[
            pltpu.VMEM((4, 512, 768), bf16),
            pltpu.VMEM((128, 512), f32),
            pltpu.VMEM(state.shape, f32),
            pltpu.SemaphoreType.DMA((4,)),
        ],
        compiler_params=params(),
    )(*operands)


def rates_of(x, state, below, beyond, metric, damping):
    row = iota((128, 128), 0)
    lane = iota((128, 128), 1)

    def differences(c):
        here = state[c, x]
        low = below[c] if x == 0 else state[c, x - 1]
        high = beyond[c] if x == 3 else state[c, x + 1]
        up = jnp.where(row < 127, pltpu.roll(here, 127, 0), 0.0)
        down = jnp.where(row > 0, pltpu.roll(here, 1, 0), 0.0)
        right = jnp.where(lane < 127, pltpu.roll(here, 127, 1), 0.0)
        left = jnp.where(lane > 0, pltpu.roll(here, 1, 1), 0.0)
        return (high - low) * 0.5, (up - down) * 0.5, (right - left) * 0.5

    def gradient(diffs, i):
        return metric[i, x] * diffs[0] + metric[3 + i, x] * diffs[1] + metric[6 + i, x] * diffs[2]

    damp = damping[x]
    pressure = -damp * state[0, x]
    for i in range(3):
        pressure = pressure - gradient(differences(1 + i), i)
    diffs = differences(0)
    return [pressure] + [-gradient(diffs, i) - damp * state[1 + i, x] for i in range(3)]


def deposit_kernel(first, *refs):
    arrived, refs = refs[0], refs[1:]
    fetched, refs = refs[:5], refs[5:]
    if first:
        low_plane, high_plane, section, counts, base, spots, cells, starts, *scratch = refs
    else:
        counts, base, spots, cells, starts, out, *scratch = refs
    slots, sorted_, total, count, now, below, beyond, metric, damping, sems = scratch
    held = (now, below, beyond, metric, damping)
    copies = [pltpu.make_async_copy(fetched[i], held[i], sems.at[i]) for i in range(5)]
    for copy in copies:
        copy.start()
    lane = iota((64, 128), 1)

    def halves(j):
        first, second = arrived[0:64, j, :], arrived[64:128, j, :]
        return (
            jnp.where(lane < 64, first, pltpu.roll(second, 64, 1)),
            jnp.where(lane < 64, pltpu.roll(first, 64, 1), second),
        )

    values = halves(0) + halves(1)
    for c in range(4):
        high, low = two_parts(values[c])
        slots[c] = high.astype(f32)
        slots[4 + c] = low.astype(f32)
    fields = 8
    if first:
        fields = 10
        label = halves(2)[0].astype(i32) - 1
        pair = jnp.where(label >= 0, label >> 15, -1)
        slots[8] = ((label >> 7) & 127).astype(f32)
        slots[9] = ((label & 127) + ((label >> 14) & 1) * 128 + 1).astype(f32)
        member = [(pair == p).astype(f32) for p in range(2)]
        sizes = [jnp.sum(m).astype(i32) for m in member]
        starts[0] = (sizes[0] + 2 * TILE - 1) // (2 * TILE)
        starts[1] = starts[0] + (sizes[1] + 2 * TILE - 1) // (2 * TILE)
        stacked = jnp.concatenate(member, axis=0).astype(bf16)
        before = exact(iota((128, 128), 0) < iota((128, 128), 1))
        inner = jnp.dot(stacked, before, preferred_element_type=f32)
        sums = [jnp.broadcast_to(jnp.sum(m, axis=1, keepdims=True), (64, 128)) for m in member]
        above = exact(iota((64, 64), 1) < iota((64, 64), 0))
        outer = jnp.dot(above, jnp.concatenate(sums, axis=1).astype(bf16), preferred_element_type=f32)
        spot = jnp.full((64, 128), -1, i32)
        for p in range(2):
            rank = (inner[p * 64 : p * 64 + 64] + outer[:, p * 128 : p * 128 + 128]).astype(i32)
            spot = jnp.where(pair == p, (starts[0] * (2 * TILE) if p else 0) + rank, spot)
        spots[...] = spot
    split, tiles = starts[0], starts[1]
    sorted_[...] = jnp.zeros_like(sorted_)
    total[...] = jnp.zeros_like(total)
    if first:
        count[...] = jnp.zeros_like(count)
    high_rows = iota((ARRIVAL_ROWS, 128), 0)
    low_rows = iota((TILE, 128), 0)
    chunk = 16

    def sort(t, _):
        spreads, places = [], []
        for j in range(chunk):
            row = pl.ds(t * chunk + j, 1)
            spot = spots[row, :]
            chosen = high_rows == (spot >> 8)
            spread = [jnp.where(chosen, slots[f, row, :], 0.0) for f in range(fields)]
            spreads.append(jnp.concatenate(spread, axis=0).astype(bf16))
            places.append(exact(low_rows == (spot & 255)))
        sorted_[...] += lax.dot_general(
            jnp.concatenate(spreads, axis=1), jnp.concatenate(places, axis=1), NT, preferred_element_type=f32
        )
        return 0

    lax.fori_loop(0, 64 // chunk, sort, 0)
    if first:
        cells[0] = sorted_[8 * ARRIVAL_ROWS : 9 * ARRIVAL_ROWS].astype(i32)
        cells[1] = sorted_[9 * ARRIVAL_ROWS : 10 * ARRIVAL_ROWS].astype(i32) - 1
    lines = iota((128, TILE), 0)
    points = iota((256, TILE), 0)

    def add(t, _):
        rows = [pl.ds(2 * t + h, 1) for h in range(2)]
        at = [lines == cells[0, row, :] for row in rows]
        selector = [exact(points == cells[1, row, :]) for row in rows]

        def spread(f):
            picked = [sorted_[pl.ds(f * ARRIVAL_ROWS + 2 * t + h, 1), :] for h in range(2)]
            return jnp.concatenate([jnp.where(at[h], picked[h], 0.0).astype(bf16) for h in range(2)], axis=1)

        high = jnp.concatenate([spread(f) for f in range(4)], axis=0)
        low = jnp.concatenate([spread(4 + f) for f in range(4)], axis=0)
        selector = jnp.concatenate(selector, axis=1)
        which = (t >= split).astype(i32)
        total[which] += lax.dot_general(
            jnp.concatenate([high, low], axis=1), jnp.concatenate([selector, selector], axis=1), NT, preferred_element_type=f32
        )
        if first:
            ones = jnp.concatenate([exact(a) for a in at], axis=1)
            count[which] += lax.dot_general(ones, selector, NT, preferred_element_type=f32)
        return 0

    lax.fori_loop(0, tiles, add, 0)
    for copy in copies:
        copy.wait()
    for x in range(4):
        lanes = slice((x % 2) * 128, (x % 2) * 128 + 128)
        if first:
            counts[x] = count[x // 2, :, lanes]
        rates = rates_of(x, now, below, beyond, metric, damping)
        for c in range(4):
            fringe = total[x // 2, c * 128 : c * 128 + 128, lanes]
            rate = rates[c] + fringe - counts[x] * now[c, x]
            if first:
                section[c, x] = now[c, x] + step_size * rate
                if x in (0, 3):
                    (low_plane if x == 0 else high_plane)[c] = section[c, x]
                base[c, x] = now[c, x] + (0.5 * step_size) * rate
            else:
                out[c, x] = base[c, x] + (0.5 * step_size) * rate


def deposit(first, arrived, *operands):
    fields = 10 if first else 8
    fetched = operands[:5]
    shape = fetched[0].shape
    if first:
        results = (
            jax.ShapeDtypeStruct((4, 128, 128), f32),
            jax.ShapeDtypeStruct((4, 128, 128), f32),
            jax.ShapeDtypeStruct(shape, f32),
            jax.ShapeDtypeStruct(shape[1:], f32),
            jax.ShapeDtypeStruct(shape, f32),
            jax.ShapeDtypeStruct((64, 128), i32),
            jax.ShapeDtypeStruct((2, ARRIVAL_ROWS, TILE), i32),
            jax.ShapeDtypeStruct((2,), i32),
        )
        specs, result_specs = placed("vhhhhh"), tuple(placed("vvvvvvvs"))
    else:
        results, result_specs = jax.ShapeDtypeStruct(shape, f32), placed("v")[0]
        specs = placed("vhhhhhvvvvs")
    return pl.pallas_call(
        functools.partial(deposit_kernel, first),
        out_shape=results,
        in_specs=specs,
        out_specs=result_specs,
        scratch_shapes=[
            pltpu.VMEM((fields, 64, 128), f32),
            pltpu.VMEM((fields * ARRIVAL_ROWS, TILE), f32),
            pltpu.VMEM((2, 512, 256), f32),
            pltpu.VMEM((2, 128, 256), f32),
        ]
        + [pltpu.VMEM(operand.shape, f32) for operand in fetched]
        + [pltpu.SemaphoreType.DMA((5,))],
        compiler_params=params(),
    )(arrived, *operands)


def neighbours(low_plane, high_plane):
    count = lax.axis_size("blk")
    forward = [(i, i + 1) for i in range(count - 1)]
    backward = [(i + 1, i) for i in range(count - 1)]
    beyond = lax.ppermute(low_plane, "blk", backward)
    below = lax.ppermute(high_plane, "blk", forward)
    return below, beyond


def exchange(outgoing):
    return lax.all_to_all(outgoing, ("grid", "blk"), split_axis=0, concat_axis=0, tiled=True)


def local(state, metric, damping, donor, fractions, dest, recept):
    state, metric, damping = state[0], metric[0], damping[0]
    fractions = fractions.reshape(3, 1, -1)
    dest = dest.reshape(1, -1)
    below, beyond = neighbours(state[:, 0], state[:, 3])
    table, labels, tiles = prepare(donor, fractions, dest, recept)
    arrived = exchange(pack(state, below, beyond, table, tiles, labels))
    low_plane, high_plane, section, *kept = deposit(True, arrived, state, below, beyond, metric, damping)
    below, beyond = neighbours(low_plane, high_plane)
    arrived = exchange(pack(section, below, beyond, table, tiles))
    return deposit(False, arrived, section, below, beyond, metric, damping, *kept)[None]


def solution(mesh):
    in_specs = (
        P("grid", None, "blk", None, None),
        P("grid", None, "blk", None, None),
        P("grid", "blk", None, None),
        P("grid", "blk"),
        P("grid", None, "blk"),
        P("grid", "blk", None),
        P("grid", "blk"),
    )
    out_specs = P("grid", None, "blk", None, None)
    return jax.shard_map(local, mesh=mesh, in_specs=in_specs, out_specs=out_specs, check_vma=False)
```

```python
import functools
import jax
import jax.numpy as jnp
from jax import lax
from jax.experimental import pallas as pl
from jax.experimental.pallas import tpu as pltpu
from jax.sharding import PartitionSpec as P

step_size = 0.4
f32, bf16, i32 = jnp.float32, jnp.bfloat16, jnp.int32
VMEM_LIMIT = 40 * 1024 * 1024
NT = (((1,), (1,)), ((), ()))


def iota(shape, dim):
    return lax.broadcasted_iota(i32, shape, dim)


def two_parts(x):
    high = x.astype(bf16)
    low = (x - high.astype(f32)).astype(bf16)
    return high, low


def params():
    return pltpu.CompilerParams(vmem_limit_bytes=VMEM_LIMIT)


TILE = 256
GROUP = 10
DONOR_ROWS = 24
RANKS = 16


def placed(kinds):
    spaces = {"v": pltpu.VMEM, "s": pltpu.SMEM, "h": pltpu.HBM}
    return [pl.BlockSpec(memory_space=spaces[kind]) for kind in kinds]


def exact(mask):
    return mask.astype(f32).astype(bf16)


def starts_of(counts):
    tiles = [(count + TILE - 1) // TILE for count in counts]
    first = tiles[0]
    second = first + tiles[1]
    third = second + tiles[2]
    return first, second, third, third + tiles[3]


def bucket_of(t, starts):
    return sum((t >= starts[i]).astype(i32) for i in range(3))


def prepare_kernel(donor, fractions, dest, recept, table, labels, starts):
    chunks = [slice(i, i + TILE) for i in range(0, donor.shape[1], TILE)]
    plane_all = donor[...] >> 14
    counts = [jnp.sum((plane_all == p + 1).astype(f32)).astype(i32) for p in range(4)]
    begin = starts_of(counts)
    for i in range(4):
        starts[i] = begin[i]
    offsets = (0,) + begin[:3]
    blocks = iota((144, TILE), 0)
    slots = iota((64, TILE), 0)
    high_rows = iota((DONOR_ROWS, TILE), 0)
    low_rows = iota((TILE, TILE), 0)
    before = exact(iota((TILE, TILE), 0) < iota((TILE, TILE), 1))
    blank = jnp.zeros((8, TILE), f32)

    members = []
    for here in chunks:
        member = (blocks == dest[:, here]) | (blocks == (donor[:, here] >> 14) + 127)
        amount = jnp.where((blocks < 128) & (recept[:, here] >= 32768), 128.0, 1.0)
        members.append(jnp.where(member, amount, 0.0))
    earlier = jnp.dot(jnp.concatenate(members, axis=0).astype(bf16), before, preferred_element_type=f32)
    counted = jnp.zeros((144, 1), f32)
    spreads, places, targets, marks = [], [], [], []
    for i, here in enumerate(chunks):
        inside = members[i] > 0.0
        ranked = jnp.where(inside, earlier[i * 144 : i * 144 + 144] + counted, 0.0)
        counted = counted + jnp.sum(members[i], axis=1, keepdims=True)
        rank = jnp.sum(ranked[:128], axis=0, keepdims=True).astype(i32)
        spot = jnp.sum(ranked[128:], axis=0, keepdims=True).astype(i32)
        label = recept[:, here]
        rank = jnp.where(label >= 32768, 63 - (rank >> 7), rank & 127)
        base = donor[:, here]
        plane = base >> 14
        offset = jnp.where(plane == 1, offsets[0], jnp.where(plane == 2, offsets[1], jnp.where(plane == 3, offsets[2], offsets[3])))
        chosen = high_rows == offset + (spot >> 8)
        fields = [(base >> 7) & 127, base & 127, dest[:, here], rank + 1]
        fields = [field.astype(f32) for field in fields]
        for k in range(3):
            rest = fractions[k, :, here]
            for _ in range(3):
                part = rest.astype(bf16).astype(f32)
                fields.append(part)
                rest = rest - part
        spread = jnp.concatenate([jnp.where(chosen, field, 0.0) for field in fields] + [blank], axis=0)
        spreads.append(spread.astype(bf16))
        places.append(exact(low_rows == (spot & 255)))
        held = slots == rank
        mark = [jnp.where(held, part.astype(f32), 0.0) for part in ((label + 1) >> 8, (label + 1) & 255)]
        marks.append(jnp.concatenate(mark, axis=0).astype(bf16))
        targets.append(exact(inside[:128]))

    def gathered(left, right):
        left, right = jnp.concatenate(left, axis=1), jnp.concatenate(right, axis=1)
        return lax.dot_general(left, right, NT, preferred_element_type=f32)

    both = gathered(targets, marks) * jnp.where(iota((128, 128), 1) < 64, 256.0, 1.0)
    labels[...] = both + pltpu.roll(both, 64, 1)
    total = gathered(spreads, places)

    def field(i):
        return total[i * DONOR_ROWS : (i + 1) * DONOR_ROWS]

    for i in range(4):
        table[i] = field(i)
    for i in range(3):
        table[4 + i] = field(4 + 3 * i) + field(5 + 3 * i) + field(6 + 3 * i)


def prepare(donor, fractions, dest, recept):
    return pl.pallas_call(
        prepare_kernel,
        out_shape=(
            jax.ShapeDtypeStruct((7, DONOR_ROWS, TILE), f32),
            jax.ShapeDtypeStruct((128, 128), f32),
            jax.ShapeDtypeStruct((4,), i32),
        ),
        in_specs=placed("vvvv"),
        out_specs=tuple(placed("vvs")),
        compiler_params=params(),
        cost_estimate=pl.CostEstimate(flops=3 * 10**9, bytes_accessed=10**6, transcendentals=0),
    )(donor, fractions, dest, recept)


def pack_kernel(with_labels, fetched, below, beyond, table, starts, *rest):
    del below
    if with_labels:
        labels, out, source, total, state, sems = rest
    else:
        out, source, total, state, sems = rest
    copies = [pltpu.make_async_copy(fetched.at[c], state.at[c], sems.at[c]) for c in range(4)]
    for copy in copies:
        copy.start()
    inner = lax.axis_index("blk") < lax.axis_size("blk") - 1
    for c in range(4):
        copies[c].wait()
        rows = slice(c * 128, c * 128 + 128)
        for x in range(5):
            high, low = two_parts(state[c, x] if x < 4 else jnp.where(inner, beyond[c], 0.0))
            for pair, side in ((x, 0), (x - 1, 128)):
                if 0 <= pair < 4:
                    for begin, part in ((0, high), (256, low), (512, high)):
                        source[pair, rows, begin + side : begin + side + 128] = part
    total[...] = jnp.zeros_like(total)
    cells = iota((128, TILE), 0)
    slots = iota((64, TILE), 0)
    begin = tuple(starts[i] for i in range(4))

    def interpolated(t):
        line, point, target, rank, fx, fy, fz = (table[i, pl.ds(t, 1), :] for i in range(7))
        line, point, target, rank = (v.astype(i32) for v in (line, point, target, rank))
        wy = jnp.where(cells == line, 1.0 - fy, jnp.where(cells == line + 1, fy, 0.0))
        wz = jnp.where(cells == point, 1.0 - fz, jnp.where(cells == point + 1, fz, 0.0))
        first, second = two_parts(wz * (1.0 - fx)), two_parts(wz * fx)
        high = [first[0], second[0]]
        weights = jnp.concatenate(high + high + [first[1], second[1]], axis=0)
        lines = jnp.dot(source[bucket_of(t, begin)], weights, preferred_element_type=f32)
        chosen = slots == rank - 1
        values = [jnp.sum(lines[c * 128 : c * 128 + 128] * wy, axis=0, keepdims=True) for c in range(4)]
        parts = []
        for which in (0, 1):
            for c in range(4):
                part = two_parts(values[c])[which].astype(f32)
                parts.append(jnp.where(chosen, part, 0.0).astype(bf16))
        return exact(cells == target), jnp.concatenate(parts, axis=0)

    def step(t, _):
        members, packed = zip(*[interpolated(t * GROUP + j) for j in range(GROUP)])
        members, packed = jnp.concatenate(members, axis=1), jnp.concatenate(packed, axis=1)
        total[...] += lax.dot_general(members, packed, NT, preferred_element_type=f32)
        return 0

    lax.fori_loop(0, (begin[3] + GROUP - 1) // GROUP, step, 0)
    for half in range(2):
        cut = slice(half * 128, half * 128 + 128)
        low = slice(256 + half * 128, 256 + half * 128 + 128)
        out[:, half, :] = total[:, cut] + total[:, low]
    if with_labels:
        out[:, 2, :] = labels[...]
        out[:, 3, :] = jnp.zeros((128, 128), f32)


def pack(state, below, beyond, table, starts, labels=None):
    first = labels is not None
    operands = (state, below, beyond, table, starts) + ((labels,) if first else ())
    return pl.pallas_call(
        functools.partial(pack_kernel, first),
        out_shape=jax.ShapeDtypeStruct((128, 4 if first else 2, 128), f32),
        in_specs=placed("hhvvsv"[: len(operands)]),
        out_specs=placed("v")[0],
        scratch_shapes=[
            pltpu.VMEM((4, 512, 768), bf16),
            pltpu.VMEM((128, 512), f32),
            pltpu.VMEM(state.shape, f32),
            pltpu.SemaphoreType.DMA((4,)),
        ],
        compiler_params=params(),
    )(*operands)


def rates_of(x, state, below, beyond, metric, damping):
    row = iota((128, 128), 0)
    lane = iota((128, 128), 1)

    block = lax.axis_index("blk")
    inner = block > 0, block < lax.axis_size("blk") - 1

    def differences(c):
        here = state[c, x]
        low = jnp.where(inner[0], below[c], 0.0) if x == 0 else state[c, x - 1]
        high = jnp.where(inner[1], beyond[c], 0.0) if x == 3 else state[c, x + 1]
        up = jnp.where(row < 127, pltpu.roll(here, 127, 0), 0.0)
        down = jnp.where(row > 0, pltpu.roll(here, 1, 0), 0.0)
        right = jnp.where(lane < 127, pltpu.roll(here, 127, 1), 0.0)
        left = jnp.where(lane > 0, pltpu.roll(here, 1, 1), 0.0)
        return (high - low) * 0.5, (up - down) * 0.5, (right - left) * 0.5

    def gradient(diffs, i):
        return metric[i, x] * diffs[0] + metric[3 + i, x] * diffs[1] + metric[6 + i, x] * diffs[2]

    damp = damping[x]
    pressure = -damp * state[0, x]
    for i in range(3):
        pressure = pressure - gradient(differences(1 + i), i)
    diffs = differences(0)
    return [pressure] + [-gradient(diffs, i) - damp * state[1 + i, x] for i in range(3)]


def deposit_kernel(first, *refs):
    arrived, refs = refs[0], refs[1:]
    fetched, refs = refs[:5], refs[5:]
    if first:
        low_plane, high_plane, section, counts, base, cells, bounds, *scratch = refs
    else:
        counts, base, cells, bounds, out, *scratch = refs
    slots, total, count, now, below, beyond, metric, damping, sems = scratch
    held = (now, below, beyond, metric, damping)
    copies = [pltpu.make_async_copy(fetched[i], held[i], sems.at[i]) for i in range(5)]
    for copy in copies:
        copy.start()
    for j in range(2):
        turned = arrived[:, j, :].T
        for half in range(2):
            high, low = two_parts(turned[half * 64 : half * 64 + 64])
            slots[2 * j + half] = high.astype(f32)
            slots[4 + 2 * j + half] = low.astype(f32)
    if first:
        label = arrived[:, 2, :].T[:64].astype(i32) - 1
        cells[0] = (label >> 7) & 127
        cells[1] = (label >> 14) * 128 + (label & 127)
        rank = iota((64, 128), 0)
        front = (label >= 0) & (label < 32768)
        bounds[0] = (jnp.max(jnp.where(front, rank + 1, 0).astype(f32)).astype(i32) + RANKS - 1) // RANKS
        bounds[1] = jnp.min(jnp.where(label >= 32768, rank, 64).astype(f32)).astype(i32) // RANKS
        count[...] = jnp.zeros_like(count)
    total[...] = jnp.zeros_like(total)
    lines = iota((128, 128), 0)
    points = iota((256, 128), 0)

    def add(pairs, t, _):
        high, low, ones, selectors = [], [], [], []
        for j in range(RANKS):
            row = pl.ds(t * RANKS + j, 1)
            at = lines == cells[0, row, :]

            def spread(f):
                return jnp.where(at, slots[f, row, :], 0.0).astype(bf16)

            high.append(jnp.concatenate([spread(f) for f in range(4)], axis=0))
            low.append(jnp.concatenate([spread(4 + f) for f in range(4)], axis=0))
            ones.append(exact(at))
            point = cells[1, row, :]
            selectors.append(jnp.concatenate([exact(points == point - 256 * p) for p in pairs], axis=0))
        selector = jnp.concatenate(selectors + selectors, axis=1)
        added = lax.dot_general(jnp.concatenate(high + low, axis=1), selector, NT, preferred_element_type=f32)
        for i, p in enumerate(pairs):
            total[p] += added[:, i * 256 : i * 256 + 256]
        if first:
            selector = jnp.concatenate(selectors, axis=1)
            added = lax.dot_general(jnp.concatenate(ones, axis=1), selector, NT, preferred_element_type=f32)
            for i, p in enumerate(pairs):
                count[p] += added[:, i * 256 : i * 256 + 256]
        return 0

    front, back = bounds[0], bounds[1]
    lower, upper = jnp.minimum(front, back), jnp.maximum(front, back)
    lax.fori_loop(0, lower, functools.partial(add, (0,)), 0)
    lax.fori_loop(lower, front, functools.partial(add, (0, 1)), 0)
    lax.fori_loop(upper, 64 // RANKS, functools.partial(add, (1,)), 0)
    for copy in copies:
        copy.wait()
    for x in range(4):
        lanes = slice((x % 2) * 128, (x % 2) * 128 + 128)
        if first:
            counts[x] = count[x // 2, :, lanes]
        rates = rates_of(x, now, below, beyond, metric, damping)
        for c in range(4):
            fringe = total[x // 2, c * 128 : c * 128 + 128, lanes]
            rate = rates[c] + fringe - counts[x] * now[c, x]
            if first:
                section[c, x] = now[c, x] + step_size * rate
                if x in (0, 3):
                    (low_plane if x == 0 else high_plane)[c] = section[c, x]
                base[c, x] = now[c, x] + (0.5 * step_size) * rate
            else:
                out[c, x] = base[c, x] + (0.5 * step_size) * rate


def deposit(first, arrived, *operands):
    fetched = operands[:5]
    shape = fetched[0].shape
    if first:
        results = (
            jax.ShapeDtypeStruct((4, 128, 128), f32),
            jax.ShapeDtypeStruct((4, 128, 128), f32),
            jax.ShapeDtypeStruct(shape, f32),
            jax.ShapeDtypeStruct(shape[1:], f32),
            jax.ShapeDtypeStruct(shape, f32),
            jax.ShapeDtypeStruct((2, 64, 128), i32),
            jax.ShapeDtypeStruct((2,), i32),
        )
        specs, result_specs = placed("vhhhhh"), tuple(placed("vvvvvvs"))
    else:
        results, result_specs = jax.ShapeDtypeStruct(shape, f32), placed("v")[0]
        specs = placed("vhhhhhvvvs")
    return pl.pallas_call(
        functools.partial(deposit_kernel, first),
        out_shape=results,
        in_specs=specs,
        out_specs=result_specs,
        scratch_shapes=[
            pltpu.VMEM((8, 64, 128), f32),
            pltpu.VMEM((2, 512, 256), f32),
            pltpu.VMEM((2, 128, 256), f32),
        ]
        + [pltpu.VMEM(operand.shape, f32) for operand in fetched]
        + [pltpu.SemaphoreType.DMA((5,))],
        compiler_params=params(),
    )(arrived, *operands)


def neighbours(low_plane, high_plane):
    count = lax.axis_size("blk")
    forward = [(i, (i + 1) % count) for i in range(count)]
    backward = [((i + 1) % count, i) for i in range(count)]
    beyond = lax.ppermute(low_plane, "blk", backward)
    below = lax.ppermute(high_plane, "blk", forward)
    return below, beyond


def exchange(outgoing):
    return lax.all_to_all(outgoing, ("grid", "blk"), split_axis=0, concat_axis=0, tiled=True)


def local(state, metric, damping, donor, fractions, dest, recept):
    state, metric, damping = state[0], metric[0], damping[0]
    fractions = fractions.reshape(3, 1, -1)
    dest = dest.reshape(1, -1)
    below, beyond = neighbours(state[:, 0], state[:, 3])
    table, labels, tiles = prepare(donor, fractions, dest, recept)
    arrived = exchange(pack(state, below, beyond, table, tiles, labels))
    low_plane, high_plane, section, *kept = deposit(True, arrived, state, below, beyond, metric, damping)
    below, beyond = neighbours(low_plane, high_plane)
    arrived = exchange(pack(section, below, beyond, table, tiles))
    return deposit(False, arrived, section, below, beyond, metric, damping, *kept)[None]


def solution(mesh):
    in_specs = (
        P("grid", None, "blk", None, None),
        P("grid", None, "blk", None, None),
        P("grid", "blk", None, None),
        P("grid", "blk"),
        P("grid", None, "blk"),
        P("grid", "blk", None),
        P("grid", "blk"),
    )
    out_specs = P("grid", None, "blk", None, None)
    return jax.shard_map(local, mesh=mesh, in_specs=in_specs, out_specs=out_specs, check_vma=False)
```

```python
import functools
import jax
import jax.numpy as jnp
from jax import lax
from jax.experimental import pallas as pl
from jax.experimental.pallas import tpu as pltpu
from jax.sharding import PartitionSpec as P

step_size = 0.4
f32, bf16, i32 = jnp.float32, jnp.bfloat16, jnp.int32
VMEM_LIMIT = 40 * 1024 * 1024
NT = (((1,), (1,)), ((), ()))


def iota(shape, dim):
    return lax.broadcasted_iota(i32, shape, dim)


def two_parts(x):
    high = x.astype(bf16)
    low = (x - high.astype(f32)).astype(bf16)
    return high, low


def params(limit=VMEM_LIMIT):
    return pltpu.CompilerParams(vmem_limit_bytes=limit)


TILE = 256
NEAR_GROUP = 8
FAR_GROUP = 5
WHOLE_GROUP = 10
DONOR_ROWS = 24
RANKS = 16


def placed(kinds):
    spaces = {"v": pltpu.VMEM, "s": pltpu.SMEM, "h": pltpu.HBM}
    return [pl.BlockSpec(memory_space=spaces[kind]) for kind in kinds]


def exact(mask):
    return mask.astype(f32).astype(bf16)


def starts_of(counts):
    tiles = [(count + TILE - 1) // TILE for count in counts]
    first = tiles[0]
    second = first + tiles[1]
    third = second + tiles[2]
    return first, second, third, third + tiles[3]


def prepare_kernel(rows, table, labels, starts, donor, dest, recept):
    for i, whole_numbers in enumerate((donor, dest, recept)):
        whole_numbers[...] = rows[i].astype(i32)
    chunks = [slice(i, i + TILE) for i in range(0, donor.shape[1], TILE)]
    plane_all = donor[...] >> 14
    counts = [jnp.sum((plane_all == p + 1).astype(f32)).astype(i32) for p in range(4)]
    begin = starts_of(counts)
    for i in range(4):
        starts[i] = begin[i]
    offsets = (0,) + begin[:3]
    blocks = iota((144, TILE), 0)
    slots = iota((64, TILE), 0)
    high_rows = iota((DONOR_ROWS, TILE), 0)
    low_rows = iota((TILE, TILE), 0)
    before = exact(iota((TILE, TILE), 0) < iota((TILE, TILE), 1))
    blank = jnp.zeros((8, TILE), f32)

    members = []
    for here in chunks:
        member = (blocks == dest[:, here]) | (blocks == (donor[:, here] >> 14) + 127)
        amount = jnp.where((blocks < 128) & (recept[:, here] >= 32768), 128.0, 1.0)
        members.append(jnp.where(member, amount, 0.0))
    earlier = jnp.dot(jnp.concatenate(members, axis=0).astype(bf16), before, preferred_element_type=f32)
    counted = jnp.zeros((144, 1), f32)
    spreads, places, targets, marks = [], [], [], []
    for i, here in enumerate(chunks):
        inside = members[i] > 0.0
        ranked = jnp.where(inside, earlier[i * 144 : i * 144 + 144] + counted, 0.0)
        counted = counted + jnp.sum(members[i], axis=1, keepdims=True)
        rank = jnp.sum(ranked[:128], axis=0, keepdims=True).astype(i32)
        spot = jnp.sum(ranked[128:], axis=0, keepdims=True).astype(i32)
        label = recept[:, here]
        rank = jnp.where(label >= 32768, 63 - (rank >> 7), rank & 127)
        base = donor[:, here]
        plane = base >> 14
        offset = jnp.where(plane == 1, offsets[0], jnp.where(plane == 2, offsets[1], jnp.where(plane == 3, offsets[2], offsets[3])))
        chosen = high_rows == offset + (spot >> 8)
        fields = [(base >> 7) & 127, base & 127, dest[:, here], rank + 1]
        fields = [field.astype(f32) for field in fields]
        for k in range(3):
            rest = rows[3 + k, :, here]
            for _ in range(3):
                part = rest.astype(bf16).astype(f32)
                fields.append(part)
                rest = rest - part
        spread = jnp.concatenate([jnp.where(chosen, field, 0.0) for field in fields] + [blank], axis=0)
        spreads.append(spread.astype(bf16))
        places.append(exact(low_rows == (spot & 255)))
        held = slots == rank
        mark = [jnp.where(held, part.astype(f32), 0.0) for part in ((label + 1) >> 8, (label + 1) & 255)]
        marks.append(jnp.concatenate(mark, axis=0).astype(bf16))
        targets.append(exact(inside[:128]))

    def gathered(left, right):
        left, right = jnp.concatenate(left, axis=1), jnp.concatenate(right, axis=1)
        return lax.dot_general(left, right, NT, preferred_element_type=f32)

    both = gathered(targets, marks) * jnp.where(iota((128, 128), 1) < 64, 256.0, 1.0)
    labels[...] = both + pltpu.roll(both, 64, 1)
    total = gathered(spreads, places)

    def field(i):
        return total[i * DONOR_ROWS : (i + 1) * DONOR_ROWS]

    for i in range(4):
        table[i] = field(i)
    for i in range(3):
        table[4 + i] = field(4 + 3 * i) + field(5 + 3 * i) + field(6 + 3 * i)


def prepare(donor, fractions, dest, recept):
    rows = [x.astype(f32).reshape(-1, 1, x.shape[-1]) for x in (donor, dest, recept, fractions)]
    rows = jnp.concatenate(rows, axis=0)
    return pl.pallas_call(
        prepare_kernel,
        out_shape=(
            jax.ShapeDtypeStruct((7, DONOR_ROWS, TILE), f32),
            jax.ShapeDtypeStruct((128, 128), f32),
            jax.ShapeDtypeStruct((4,), i32),
        ),
        in_specs=placed("v"),
        out_specs=tuple(placed("vvs")),
        scratch_shapes=[pltpu.VMEM(donor.shape, i32)] * 3,
        compiler_params=params(),
        cost_estimate=pl.CostEstimate(flops=3 * 10**9, bytes_accessed=10**6, transcendentals=0),
    )(rows)


def pack_kernel(far, with_labels, *refs):
    if far:
        fetched, _, beyond, table, starts, given, out, source, total, state, sems = refs
        held = fetched if with_labels else fetched.at[:, 3:4]
        copies = [pltpu.make_async_copy(held.at[c], state.at[c], sems.at[c]) for c in range(4)]
    else:
        fetched, table, starts, total, source, state, sems = refs
        copies = [pltpu.make_async_copy(fetched.at[c], state.at[c], sems.at[c]) for c in range(4)]
    for copy in copies:
        copy.start()
    inner = lax.axis_index("blk") < lax.axis_size("blk") - 1
    planes = state.shape[1]
    for c in range(4):
        copies[c].wait()
        rows = slice(c * 128, c * 128 + 128)
        for x in range(planes + far):
            high, low = two_parts(state[c, x] if x < planes else jnp.where(inner, beyond[c], 0.0))
            source[0, rows, x * 128 : x * 128 + 128] = high
            source[1, rows, x * 128 : x * 128 + 128] = low
    total[...] = given[...] if far and not with_labels else jnp.zeros_like(total)
    cells = iota((128, TILE), 0)
    slots = iota((64, TILE), 0)
    first = starts[2] if far and not with_labels else 0
    last = starts[3] if far else starts[2]
    group = WHOLE_GROUP if with_labels else FAR_GROUP if far else NEAR_GROUP
    inside = 3 if with_labels else 0 if far else 2

    def interpolated(t):
        line, point, target, rank, fx, fy, fz = (table[i, pl.ds(t, 1), :] for i in range(7))
        line, point, target, rank = (v.astype(i32) for v in (line, point, target, rank))
        wy = jnp.where(cells == line, 1.0 - fy, jnp.where(cells == line + 1, fy, 0.0))
        wz = jnp.where(cells == point, 1.0 - fz, jnp.where(cells == point + 1, fz, 0.0))
        lower, upper = two_parts(wz * (1.0 - fx)), two_parts(wz * fx)
        high = [lower[0], upper[0]]
        weights = jnp.concatenate(high + high + [lower[1], upper[1]], axis=0)
        pair = sum((t >= starts[i]).astype(i32) for i in range(inside))
        both = pl.ds(pl.multiple_of(pair * 128, 128), 256) if inside else slice(0, 256)
        high, low = source[0, :, both], source[1, :, both]
        lines = jnp.dot(jnp.concatenate([high, low, high], axis=1), weights, preferred_element_type=f32)
        chosen = slots == jnp.where(t < last, rank - 1, -1)
        values = [jnp.sum(lines[c * 128 : c * 128 + 128] * wy, axis=0, keepdims=True) for c in range(4)]
        parts = []
        for which in (0, 1):
            for c in range(4):
                part = two_parts(values[c])[which].astype(f32)
                parts.append(jnp.where(chosen, part, 0.0).astype(bf16))
        return exact(cells == target), jnp.concatenate(parts, axis=0)

    def step(t, _):
        members, packed = zip(*[interpolated(first + t * group + j) for j in range(group)])
        members, packed = jnp.concatenate(members, axis=1), jnp.concatenate(packed, axis=1)
        total[...] += lax.dot_general(members, packed, NT, preferred_element_type=f32)
        return 0

    lax.fori_loop(0, (last - first + group - 1) // group, step, 0)
    if not far:
        return
    for half in range(2):
        cut = slice(half * 128, half * 128 + 128)
        low = slice(256 + half * 128, 256 + half * 128 + 128)
        out[:, 0, cut] = total[:, cut] + total[:, low]
    if with_labels:
        out[:, 0, 256:384] = given[...]


def pack_near(state, table, starts):
    return pl.pallas_call(
        functools.partial(pack_kernel, 0, False),
        out_shape=jax.ShapeDtypeStruct((128, 512), f32),
        in_specs=placed("hvs"),
        out_specs=placed("v")[0],
        scratch_shapes=[
            pltpu.VMEM((2, 512, 512), bf16),
            pltpu.VMEM(state.shape, f32),
            pltpu.SemaphoreType.DMA((4,)),
        ],
        compiler_params=params(),
        cost_estimate=pl.CostEstimate(flops=5 * 10**9, bytes_accessed=10**6, transcendentals=0),
    )(state, table, starts)


def pack_rest(first, state, below, beyond, table, starts, given):
    planes = 4 if first else 1
    return pl.pallas_call(
        functools.partial(pack_kernel, 1, first),
        out_shape=jax.ShapeDtypeStruct((128, 1, 384 if first else 256), f32),
        in_specs=placed("hhvvsv"),
        out_specs=placed("v")[0],
        scratch_shapes=[
            pltpu.VMEM((2, 512, planes * 128 + 128), bf16),
            pltpu.VMEM((128, 512), f32),
            pltpu.VMEM((4, planes, 128, 128), f32),
            pltpu.SemaphoreType.DMA((4,)),
        ],
        compiler_params=params(),
    )(state, below, beyond, table, starts, given)


def rates_of(x, state, below, beyond, metric, damping):
    row = iota((128, 128), 0)
    lane = iota((128, 128), 1)

    block = lax.axis_index("blk")
    inner = block > 0, block < lax.axis_size("blk") - 1

    def differences(c):
        here = state[c, x]
        low = jnp.where(inner[0], below[c], 0.0) if x == 0 else state[c, x - 1]
        high = jnp.where(inner[1], beyond[c], 0.0) if x == 3 else state[c, x + 1]
        up = jnp.where(row < 127, pltpu.roll(here, 127, 0), 0.0)
        down = jnp.where(row > 0, pltpu.roll(here, 1, 0), 0.0)
        right = jnp.where(lane < 127, pltpu.roll(here, 127, 1), 0.0)
        left = jnp.where(lane > 0, pltpu.roll(here, 1, 1), 0.0)
        return (high - low) * 0.5, (up - down) * 0.5, (right - left) * 0.5

    def gradient(diffs, i):
        return metric[i, x] * diffs[0] + metric[3 + i, x] * diffs[1] + metric[6 + i, x] * diffs[2]

    damp = damping[x]
    pressure = -damp * state[0, x]
    for i in range(3):
        pressure = pressure - gradient(differences(1 + i), i)
    diffs = differences(0)
    return [pressure] + [-gradient(diffs, i) - damp * state[1 + i, x] for i in range(3)]


def deposit_kernel(first, *refs):
    fetches = 5 if first else 6
    arrived, fetched, refs = refs[0], refs[1 : fetches + 1], refs[fetches + 1 :]
    if first:
        low_plane, high_plane, out, counts, cells, bounds, *scratch = refs
    else:
        counts, cells, bounds, out, *scratch = refs
    slots, total, count, sems, *held = scratch
    now, below, beyond, metric, damping = held[:5]
    copies = [pltpu.make_async_copy(fetched[i], held[i], sems.at[i]) for i in range(fetches)]
    for copy in copies:
        copy.start()
    for j in range(2):
        turned = arrived[:, 0, j * 128 : j * 128 + 128].T
        for half in range(2):
            high, low = two_parts(turned[half * 64 : half * 64 + 64])
            slots[2 * j + half] = high.astype(f32)
            slots[4 + 2 * j + half] = low.astype(f32)
    if first:
        label = arrived[:, 0, 256:384].T[:64].astype(i32) - 1
        cells[0] = (label >> 7) & 127
        cells[1] = (label >> 14) * 128 + (label & 127)
        rank = iota((64, 128), 0)
        front = (label >= 0) & (label < 32768)
        bounds[0] = (jnp.max(jnp.where(front, rank + 1, 0).astype(f32)).astype(i32) + RANKS - 1) // RANKS
        bounds[1] = jnp.min(jnp.where(label >= 32768, rank, 64).astype(f32)).astype(i32) // RANKS
        count[...] = jnp.zeros_like(count)
    total[...] = jnp.zeros_like(total)
    lines = iota((128, 128), 0)
    points = iota((256, 128), 0)

    def add(pairs, t, _):
        high, low, ones, selectors = [], [], [], []
        for j in range(RANKS):
            row = pl.ds(t * RANKS + j, 1)
            at = lines == cells[0, row, :]

            def spread(f):
                return jnp.where(at, slots[f, row, :], 0.0).astype(bf16)

            high.append(jnp.concatenate([spread(f) for f in range(4)], axis=0))
            low.append(jnp.concatenate([spread(4 + f) for f in range(4)], axis=0))
            ones.append(exact(at))
            point = cells[1, row, :]
            selectors.append(jnp.concatenate([exact(points == point - 256 * p) for p in pairs], axis=0))
        selector = jnp.concatenate(selectors + selectors, axis=1)
        added = lax.dot_general(jnp.concatenate(high + low, axis=1), selector, NT, preferred_element_type=f32)
        for i, p in enumerate(pairs):
            total[p] += added[:, i * 256 : i * 256 + 256]
        if first:
            selector = jnp.concatenate(selectors, axis=1)
            added = lax.dot_general(jnp.concatenate(ones, axis=1), selector, NT, preferred_element_type=f32)
            for i, p in enumerate(pairs):
                count[p] += added[:, i * 256 : i * 256 + 256]
        return 0

    front, back = bounds[0], bounds[1]
    lower, upper = jnp.minimum(front, back), jnp.maximum(front, back)
    lax.fori_loop(0, lower, functools.partial(add, (0,)), 0)
    lax.fori_loop(lower, front, functools.partial(add, (0, 1)), 0)
    lax.fori_loop(upper, 64 // RANKS, functools.partial(add, (1,)), 0)
    for copy in copies:
        copy.wait()
    for x in range(4):
        lanes = slice((x % 2) * 128, (x % 2) * 128 + 128)
        if first:
            counts[x] = count[x // 2, :, lanes]
        rates = rates_of(x, now, below, beyond, metric, damping)
        for c in range(4):
            fringe = total[x // 2, c * 128 : c * 128 + 128, lanes]
            rate = rates[c] + fringe - counts[x] * now[c, x]
            if first:
                out[c, x] = now[c, x] + step_size * rate
                if x in (0, 3):
                    (low_plane if x == 0 else high_plane)[c] = out[c, x]
            else:
                out[c, x] = 0.5 * (held[5][c, x] + now[c, x]) + (0.5 * step_size) * rate


def deposit(first, arrived, *operands):
    fetched = operands[: 5 if first else 6]
    shape = fetched[0].shape
    if first:
        results = (
            jax.ShapeDtypeStruct((4, 128, 128), f32),
            jax.ShapeDtypeStruct((4, 128, 128), f32),
            jax.ShapeDtypeStruct(shape, f32),
            jax.ShapeDtypeStruct(shape[1:], f32),
            jax.ShapeDtypeStruct((2, 64, 128), i32),
            jax.ShapeDtypeStruct((2,), i32),
        )
        specs, result_specs = placed("vhhhhh"), tuple(placed("vvvvvs"))
    else:
        results, result_specs = jax.ShapeDtypeStruct(shape, f32), placed("v")[0]
        specs = placed("vhhhhhhvvs")
    return pl.pallas_call(
        functools.partial(deposit_kernel, first),
        out_shape=results,
        in_specs=specs,
        out_specs=result_specs,
        scratch_shapes=[
            pltpu.VMEM((8, 64, 128), f32),
            pltpu.VMEM((2, 512, 256), f32),
            pltpu.VMEM((2, 128, 256), f32),
            pltpu.SemaphoreType.DMA((len(fetched),)),
        ]
        + [pltpu.VMEM(operand.shape, f32) for operand in fetched],
        compiler_params=params(),
    )(arrived, *operands)


def neighbours(low_plane, high_plane):
    count = lax.axis_size("blk")
    forward = [(i, (i + 1) % count) for i in range(count)]
    backward = [((i + 1) % count, i) for i in range(count)]
    beyond = lax.ppermute(low_plane, "blk", backward)
    below = lax.ppermute(high_plane, "blk", forward)
    return below, beyond


def exchange(outgoing):
    return lax.all_to_all(outgoing, ("grid", "blk"), split_axis=0, concat_axis=0, tiled=True)


def local(state, metric, damping, donor, fractions, dest, recept):
    state, metric, damping = state[0], metric[0], damping[0]
    fractions = fractions.reshape(3, 1, -1)
    dest = dest.reshape(1, -1)
    below, beyond = neighbours(state[:, 0], state[:, 3])
    table, labels, tiles = prepare(donor, fractions, dest, recept)
    arrived = exchange(pack_rest(True, state, below, beyond, table, tiles, labels))
    low_plane, high_plane, section, *kept = deposit(True, arrived, state, below, beyond, metric, damping)
    below, beyond = neighbours(low_plane, high_plane)
    partial = pack_near(section, table, tiles)
    arrived = exchange(pack_rest(False, section, below, beyond, table, tiles, partial))
    return deposit(False, arrived, section, below, beyond, metric, damping, state, *kept)[None]


def solution(mesh):
    in_specs = (
        P("grid", None, "blk", None, None),
        P("grid", None, "blk", None, None),
        P("grid", "blk", None, None),
        P("grid", "blk"),
        P("grid", None, "blk"),
        P("grid", "blk", None),
        P("grid", "blk"),
    )
    out_specs = P("grid", None, "blk", None, None)
    return jax.shard_map(local, mesh=mesh, in_specs=in_specs, out_specs=out_specs, check_vma=False)
```

```python
import functools
import jax
import jax.numpy as jnp
from jax import lax
from jax.experimental import pallas as pl
from jax.experimental.pallas import tpu as pltpu
from jax.sharding import PartitionSpec as P

step_size = 0.4
f32, bf16, i32 = jnp.float32, jnp.bfloat16, jnp.int32
VMEM_LIMIT = 40 * 1024 * 1024
NT = (((1,), (1,)), ((), ()))


def iota(shape, dim):
    return lax.broadcasted_iota(i32, shape, dim)


def two_parts(x):
    high = x.astype(bf16)
    low = (x - high.astype(f32)).astype(bf16)
    return high, low


def params(limit=VMEM_LIMIT):
    return pltpu.CompilerParams(vmem_limit_bytes=limit)


TILE = 256
NEAR_GROUP = 8
FAR_GROUP = 5
WHOLE_GROUP = 10
DONOR_ROWS = 24
RANKS = 16


def placed(kinds):
    spaces = {"v": pltpu.VMEM, "s": pltpu.SMEM, "h": pltpu.HBM}
    return [pl.BlockSpec(memory_space=spaces[kind]) for kind in kinds]


def exact(mask):
    return mask.astype(f32).astype(bf16)


def starts_of(counts):
    tiles = [(count + TILE - 1) // TILE for count in counts]
    first = tiles[0]
    second = first + tiles[1]
    third = second + tiles[2]
    return first, second, third, third + tiles[3]


def prepare_kernel(numbers, fractions, table, labels, starts):
    donor, dest, recept = numbers.at[0], numbers.at[1], numbers.at[2]
    chunks = [slice(i, i + TILE) for i in range(0, donor.shape[1], TILE)]
    plane_all = donor[...] >> 14
    counts = [jnp.sum((plane_all == p + 1).astype(f32)).astype(i32) for p in range(4)]
    begin = starts_of(counts)
    for i in range(4):
        starts[i] = begin[i]
    offsets = (0,) + begin[:3]
    blocks = iota((144, TILE), 0)
    slots = iota((64, TILE), 0)
    high_rows = iota((DONOR_ROWS, TILE), 0)
    low_rows = iota((TILE, TILE), 0)
    before = exact(iota((TILE, TILE), 0) < iota((TILE, TILE), 1))
    blank = jnp.zeros((8, TILE), f32)

    members = []
    for here in chunks:
        member = (blocks == dest[:, here]) | (blocks == (donor[:, here] >> 14) + 127)
        amount = jnp.where((blocks < 128) & (recept[:, here] >= 32768), 128.0, 1.0)
        members.append(jnp.where(member, amount, 0.0))
    earlier = jnp.dot(jnp.concatenate(members, axis=0).astype(bf16), before, preferred_element_type=f32)
    counted = jnp.zeros((144, 1), f32)
    spreads, places, targets, marks = [], [], [], []
    for i, here in enumerate(chunks):
        inside = members[i] > 0.0
        ranked = jnp.where(inside, earlier[i * 144 : i * 144 + 144] + counted, 0.0)
        counted = counted + jnp.sum(members[i], axis=1, keepdims=True)
        rank = jnp.sum(ranked[:128], axis=0, keepdims=True).astype(i32)
        spot = jnp.sum(ranked[128:], axis=0, keepdims=True).astype(i32)
        label = recept[:, here]
        rank = jnp.where(label >= 32768, 63 - (rank >> 7), rank & 127)
        base = donor[:, here]
        plane = base >> 14
        offset = jnp.where(plane == 1, offsets[0], jnp.where(plane == 2, offsets[1], jnp.where(plane == 3, offsets[2], offsets[3])))
        chosen = high_rows == offset + (spot >> 8)
        fields = [(base >> 7) & 127, base & 127, dest[:, here], rank + 1]
        fields = [field.astype(f32) for field in fields]
        for k in range(3):
            rest = fractions[k, :, here]
            for _ in range(3):
                part = rest.astype(bf16).astype(f32)
                fields.append(part)
                rest = rest - part
        spread = jnp.concatenate([jnp.where(chosen, field, 0.0) for field in fields] + [blank], axis=0)
        spreads.append(spread.astype(bf16))
        places.append(exact(low_rows == (spot & 255)))
        held = slots == rank
        mark = [jnp.where(held, part.astype(f32), 0.0) for part in ((label + 1) >> 8, (label + 1) & 255)]
        marks.append(jnp.concatenate(mark, axis=0).astype(bf16))
        targets.append(exact(inside[:128]))

    def gathered(left, right):
        left, right = jnp.concatenate(left, axis=1), jnp.concatenate(right, axis=1)
        return lax.dot_general(left, right, NT, preferred_element_type=f32)

    both = gathered(targets, marks) * jnp.where(iota((128, 128), 1) < 64, 256.0, 1.0)
    labels[...] = both + pltpu.roll(both, 64, 1)
    total = gathered(spreads, places)

    def field(i):
        return total[i * DONOR_ROWS : (i + 1) * DONOR_ROWS]

    for i in range(4):
        table[i] = field(i)
    for i in range(3):
        table[4 + i] = field(4 + 3 * i) + field(5 + 3 * i) + field(6 + 3 * i)


def prepare(donor, fractions, dest, recept):
    numbers = jnp.concatenate([x.reshape(1, 1, -1) for x in (donor, dest, recept)], axis=0)
    return pl.pallas_call(
        prepare_kernel,
        out_shape=(
            jax.ShapeDtypeStruct((7, DONOR_ROWS, TILE), f32),
            jax.ShapeDtypeStruct((128, 128), f32),
            jax.ShapeDtypeStruct((4,), i32),
        ),
        in_specs=placed("vv"),
        out_specs=tuple(placed("vvs")),
        compiler_params=params(),
        cost_estimate=pl.CostEstimate(flops=3 * 10**9, bytes_accessed=10**6, transcendentals=0),
    )(numbers, fractions)


def pack_kernel(far, with_labels, *refs):
    if far:
        fetched, _, beyond, table, starts, given, out, source, total, state, sems = refs
        held = fetched if with_labels else fetched.at[:, 3:4]
        copies = [pltpu.make_async_copy(held.at[c], state.at[c], sems.at[c]) for c in range(4)]
    else:
        fetched, table, starts, total, source, state, sems = refs
        copies = [pltpu.make_async_copy(fetched.at[c], state.at[c], sems.at[c]) for c in range(4)]
    for copy in copies:
        copy.start()
    inner = lax.axis_index("blk") < lax.axis_size("blk") - 1
    planes = state.shape[1]
    for c in range(4):
        copies[c].wait()
        rows = slice(c * 128, c * 128 + 128)
        for x in range(planes + far):
            high, low = two_parts(state[c, x] if x < planes else jnp.where(inner, beyond[c], 0.0))
            source[0, rows, x * 128 : x * 128 + 128] = high
            source[1, rows, x * 128 : x * 128 + 128] = low
    total[...] = given[...] if far and not with_labels else jnp.zeros_like(total)
    cells = iota((128, TILE), 0)
    slots = iota((64, TILE), 0)
    first = starts[2] if far and not with_labels else 0
    last = starts[3] if far else starts[2]
    group = WHOLE_GROUP if with_labels else FAR_GROUP if far else NEAR_GROUP
    inside = 3 if with_labels else 0 if far else 2

    def interpolated(t):
        line, point, target, rank, fx, fy, fz = (table[i, pl.ds(t, 1), :] for i in range(7))
        line, point, target, rank = (v.astype(i32) for v in (line, point, target, rank))
        wy = jnp.where(cells == line, 1.0 - fy, jnp.where(cells == line + 1, fy, 0.0))
        wz = jnp.where(cells == point, 1.0 - fz, jnp.where(cells == point + 1, fz, 0.0))
        lower, upper = two_parts(wz * (1.0 - fx)), two_parts(wz * fx)
        high = [lower[0], upper[0]]
        weights = jnp.concatenate(high + high + [lower[1], upper[1]], axis=0)
        pair = sum((t >= starts[i]).astype(i32) for i in range(inside))
        both = pl.ds(pl.multiple_of(pair * 128, 128), 256) if inside else slice(0, 256)
        high, low = source[0, :, both], source[1, :, both]
        lines = jnp.dot(jnp.concatenate([high, low, high], axis=1), weights, preferred_element_type=f32)
        chosen = slots == jnp.where(t < last, rank - 1, -1)
        values = [jnp.sum(lines[c * 128 : c * 128 + 128] * wy, axis=0, keepdims=True) for c in range(4)]
        parts = []
        for which in (0, 1):
            for c in range(4):
                part = two_parts(values[c])[which].astype(f32)
                parts.append(jnp.where(chosen, part, 0.0).astype(bf16))
        return exact(cells == target), jnp.concatenate(parts, axis=0)

    def step(t, _):
        members, packed = zip(*[interpolated(first + t * group + j) for j in range(group)])
        members, packed = jnp.concatenate(members, axis=1), jnp.concatenate(packed, axis=1)
        total[...] += lax.dot_general(members, packed, NT, preferred_element_type=f32)
        return 0

    lax.fori_loop(0, (last - first + group - 1) // group, step, 0)
    if not far:
        return
    for half in range(2):
        cut = slice(half * 128, half * 128 + 128)
        low = slice(256 + half * 128, 256 + half * 128 + 128)
        out[:, 0, cut] = total[:, cut] + total[:, low]
    if with_labels:
        out[:, 0, 256:384] = given[...]


def pack_near(state, table, starts):
    return pl.pallas_call(
        functools.partial(pack_kernel, 0, False),
        out_shape=jax.ShapeDtypeStruct((128, 512), f32),
        in_specs=placed("hvs"),
        out_specs=placed("v")[0],
        scratch_shapes=[
            pltpu.VMEM((2, 512, 512), bf16),
            pltpu.VMEM(state.shape, f32),
            pltpu.SemaphoreType.DMA((4,)),
        ],
        compiler_params=params(),
        cost_estimate=pl.CostEstimate(flops=5 * 10**9, bytes_accessed=10**6, transcendentals=0),
    )(state, table, starts)


def pack_rest(first, state, below, beyond, table, starts, given):
    planes = 4 if first else 1
    return pl.pallas_call(
        functools.partial(pack_kernel, 1, first),
        out_shape=jax.ShapeDtypeStruct((128, 1, 384 if first else 256), f32),
        in_specs=placed("hhvvsv"),
        out_specs=placed("v")[0],
        scratch_shapes=[
            pltpu.VMEM((2, 512, planes * 128 + 128), bf16),
            pltpu.VMEM((128, 512), f32),
            pltpu.VMEM((4, planes, 128, 128), f32),
            pltpu.SemaphoreType.DMA((4,)),
        ],
        compiler_params=params(),
    )(state, below, beyond, table, starts, given)


def rates_of(x, state, below, beyond, metric, damping):
    row = iota((128, 128), 0)
    lane = iota((128, 128), 1)

    block = lax.axis_index("blk")
    inner = block > 0, block < lax.axis_size("blk") - 1

    def differences(c):
        here = state[c, x]
        low = jnp.where(inner[0], below[c], 0.0) if x == 0 else state[c, x - 1]
        high = jnp.where(inner[1], beyond[c], 0.0) if x == 3 else state[c, x + 1]
        up = jnp.where(row < 127, pltpu.roll(here, 127, 0), 0.0)
        down = jnp.where(row > 0, pltpu.roll(here, 1, 0), 0.0)
        right = jnp.where(lane < 127, pltpu.roll(here, 127, 1), 0.0)
        left = jnp.where(lane > 0, pltpu.roll(here, 1, 1), 0.0)
        return (high - low) * 0.5, (up - down) * 0.5, (right - left) * 0.5

    def gradient(diffs, i):
        return metric[i, x] * diffs[0] + metric[3 + i, x] * diffs[1] + metric[6 + i, x] * diffs[2]

    damp = damping[x]
    pressure = -damp * state[0, x]
    for i in range(3):
        pressure = pressure - gradient(differences(1 + i), i)
    diffs = differences(0)
    return [pressure] + [-gradient(diffs, i) - damp * state[1 + i, x] for i in range(3)]


def deposit_kernel(first, *refs):
    fetches = 5 if first else 6
    arrived, fetched, refs = refs[0], refs[1 : fetches + 1], refs[fetches + 1 :]
    if first:
        low_plane, high_plane, out, counts, cells, bounds, *scratch = refs
    else:
        counts, cells, bounds, out, *scratch = refs
    slots, total, count, sems, *held = scratch
    now, below, beyond, metric, damping = held[:5]
    copies = [pltpu.make_async_copy(fetched[i], held[i], sems.at[i]) for i in range(fetches)]
    for copy in copies:
        copy.start()
    for j in range(2):
        turned = arrived[:, 0, j * 128 : j * 128 + 128].T
        for half in range(2):
            high, low = two_parts(turned[half * 64 : half * 64 + 64])
            slots[2 * j + half] = high.astype(f32)
            slots[4 + 2 * j + half] = low.astype(f32)
    if first:
        label = arrived[:, 0, 256:384].T[:64].astype(i32) - 1
        cells[0] = (label >> 7) & 127
        cells[1] = (label >> 14) * 128 + (label & 127)
        rank = iota((64, 128), 0)
        front = (label >= 0) & (label < 32768)
        bounds[0] = (jnp.max(jnp.where(front, rank + 1, 0).astype(f32)).astype(i32) + RANKS - 1) // RANKS
        bounds[1] = jnp.min(jnp.where(label >= 32768, rank, 64).astype(f32)).astype(i32) // RANKS
        count[...] = jnp.zeros_like(count)
    total[...] = jnp.zeros_like(total)
    lines = iota((128, 128), 0)
    points = iota((256, 128), 0)

    def add(pairs, t, _):
        high, low, ones, selectors = [], [], [], []
        for j in range(RANKS):
            row = pl.ds(t * RANKS + j, 1)
            at = lines == cells[0, row, :]

            def spread(f):
                return jnp.where(at, slots[f, row, :], 0.0).astype(bf16)

            high.append(jnp.concatenate([spread(f) for f in range(4)], axis=0))
            low.append(jnp.concatenate([spread(4 + f) for f in range(4)], axis=0))
            ones.append(exact(at))
            point = cells[1, row, :]
            selectors.append(jnp.concatenate([exact(points == point - 256 * p) for p in pairs], axis=0))
        selector = jnp.concatenate(selectors + selectors, axis=1)
        added = lax.dot_general(jnp.concatenate(high + low, axis=1), selector, NT, preferred_element_type=f32)
        for i, p in enumerate(pairs):
            total[p] += added[:, i * 256 : i * 256 + 256]
        if first:
            selector = jnp.concatenate(selectors, axis=1)
            added = lax.dot_general(jnp.concatenate(ones, axis=1), selector, NT, preferred_element_type=f32)
            for i, p in enumerate(pairs):
                count[p] += added[:, i * 256 : i * 256 + 256]
        return 0

    front, back = bounds[0], bounds[1]
    lower, upper = jnp.minimum(front, back), jnp.maximum(front, back)
    lax.fori_loop(0, lower, functools.partial(add, (0,)), 0)
    lax.fori_loop(lower, front, functools.partial(add, (0, 1)), 0)
    lax.fori_loop(upper, 64 // RANKS, functools.partial(add, (1,)), 0)
    for copy in copies:
        copy.wait()
    for x in range(4):
        lanes = slice((x % 2) * 128, (x % 2) * 128 + 128)
        if first:
            counts[x] = count[x // 2, :, lanes]
        rates = rates_of(x, now, below, beyond, metric, damping)
        for c in range(4):
            fringe = total[x // 2, c * 128 : c * 128 + 128, lanes]
            rate = rates[c] + fringe - counts[x] * now[c, x]
            if first:
                out[c, x] = now[c, x] + step_size * rate
                if x in (0, 3):
                    (low_plane if x == 0 else high_plane)[c] = out[c, x]
            else:
                out[c, x] = 0.5 * (held[5][c, x] + now[c, x]) + (0.5 * step_size) * rate


def deposit(first, arrived, *operands):
    fetched = operands[: 5 if first else 6]
    shape = fetched[0].shape
    if first:
        results = (
            jax.ShapeDtypeStruct((4, 128, 128), f32),
            jax.ShapeDtypeStruct((4, 128, 128), f32),
            jax.ShapeDtypeStruct(shape, f32),
            jax.ShapeDtypeStruct(shape[1:], f32),
            jax.ShapeDtypeStruct((2, 64, 128), i32),
            jax.ShapeDtypeStruct((2,), i32),
        )
        specs, result_specs = placed("vhhhhh"), tuple(placed("vvvvvs"))
    else:
        results, result_specs = jax.ShapeDtypeStruct(shape, f32), placed("v")[0]
        specs = placed("vhhhhhhvvs")
    return pl.pallas_call(
        functools.partial(deposit_kernel, first),
        out_shape=results,
        in_specs=specs,
        out_specs=result_specs,
        scratch_shapes=[
            pltpu.VMEM((8, 64, 128), f32),
            pltpu.VMEM((2, 512, 256), f32),
            pltpu.VMEM((2, 128, 256), f32),
            pltpu.SemaphoreType.DMA((len(fetched),)),
        ]
        + [pltpu.VMEM(operand.shape, f32) for operand in fetched],
        compiler_params=params(),
    )(arrived, *operands)


def neighbours(low_plane, high_plane):
    count = lax.axis_size("blk")
    forward = [(i, (i + 1) % count) for i in range(count)]
    backward = [((i + 1) % count, i) for i in range(count)]
    beyond = lax.ppermute(low_plane, "blk", backward)
    below = lax.ppermute(high_plane, "blk", forward)
    return below, beyond


def exchange(outgoing):
    return lax.all_to_all(outgoing, ("grid", "blk"), split_axis=0, concat_axis=0, tiled=True)


def local(state, metric, damping, donor, fractions, dest, recept):
    state, metric, damping = state[0], metric[0], damping[0]
    fractions = fractions.reshape(3, 1, -1)
    dest = dest.reshape(1, -1)
    below, beyond = neighbours(state[:, 0], state[:, 3])
    table, labels, tiles = prepare(donor, fractions, dest, recept)
    arrived = exchange(pack_rest(True, state, below, beyond, table, tiles, labels))
    low_plane, high_plane, section, *kept = deposit(True, arrived, state, below, beyond, metric, damping)
    below, beyond = neighbours(low_plane, high_plane)
    partial = pack_near(section, table, tiles)
    arrived = exchange(pack_rest(False, section, below, beyond, table, tiles, partial))
    return deposit(False, arrived, section, below, beyond, metric, damping, state, *kept)[None]


def solution(mesh):
    in_specs = (
        P("grid", None, "blk", None, None),
        P("grid", None, "blk", None, None),
        P("grid", "blk", None, None),
        P("grid", "blk"),
        P("grid", None, "blk"),
        P("grid", "blk", None),
        P("grid", "blk"),
    )
    out_specs = P("grid", None, "blk", None, None)
    return jax.shard_map(local, mesh=mesh, in_specs=in_specs, out_specs=out_specs, check_vma=False)
```

```python
import functools
import jax
import jax.numpy as jnp
from jax import lax
from jax.experimental import pallas as pl
from jax.experimental.pallas import tpu as pltpu
from jax.sharding import PartitionSpec as P

step_size = 0.4
f32, bf16, i32 = jnp.float32, jnp.bfloat16, jnp.int32
VMEM_LIMIT = 40 * 1024 * 1024
NT = (((1,), (1,)), ((), ()))


def iota(shape, dim):
    return lax.broadcasted_iota(i32, shape, dim)


def two_parts(x):
    high = x.astype(bf16)
    low = (x - high.astype(f32)).astype(bf16)
    return high, low


def params(limit=VMEM_LIMIT):
    return pltpu.CompilerParams(vmem_limit_bytes=limit)


TILE = 256
NEAR_GROUP = 8
FAR_GROUP = 5
WHOLE_GROUP = 20
DONOR_ROWS = 24
RANKS = 16


def placed(kinds):
    spaces = {"v": pltpu.VMEM, "s": pltpu.SMEM, "h": pltpu.HBM}
    return [pl.BlockSpec(memory_space=spaces[kind]) for kind in kinds]


def exact(mask):
    return mask.astype(f32).astype(bf16)


def starts_of(counts):
    tiles = [(count + TILE - 1) // TILE for count in counts]
    first = tiles[0]
    second = first + tiles[1]
    third = second + tiles[2]
    return first, second, third, third + tiles[3]


def prepare_kernel(numbers, fractions, table, labels, starts):
    donor, dest, recept = numbers.at[0], numbers.at[1], numbers.at[2]
    chunks = [slice(i, i + TILE) for i in range(0, donor.shape[1], TILE)]
    plane_all = donor[...] >> 14
    counts = [jnp.sum((plane_all == p + 1).astype(f32)).astype(i32) for p in range(4)]
    begin = starts_of(counts)
    for i in range(4):
        starts[i] = begin[i]
    offsets = (0,) + begin[:3]
    blocks = iota((144, TILE), 0)
    slots = iota((64, TILE), 0)
    high_rows = iota((DONOR_ROWS, TILE), 0)
    low_rows = iota((TILE, TILE), 0)
    before = exact(iota((TILE, TILE), 0) < iota((TILE, TILE), 1))
    blank = jnp.zeros((8, TILE), f32)

    members = []
    for here in chunks:
        member = (blocks == dest[:, here]) | (blocks == (donor[:, here] >> 14) + 127)
        amount = jnp.where((blocks < 128) & (recept[:, here] >= 32768), 128.0, 1.0)
        members.append(jnp.where(member, amount, 0.0))
    earlier = jnp.dot(jnp.concatenate(members, axis=0).astype(bf16), before, preferred_element_type=f32)
    counted = jnp.zeros((144, 1), f32)
    spreads, places, targets, marks = [], [], [], []
    for i, here in enumerate(chunks):
        inside = members[i] > 0.0
        ranked = jnp.where(inside, earlier[i * 144 : i * 144 + 144] + counted, 0.0)
        counted = counted + jnp.sum(members[i], axis=1, keepdims=True)
        rank = jnp.sum(ranked[:128], axis=0, keepdims=True).astype(i32)
        spot = jnp.sum(ranked[128:], axis=0, keepdims=True).astype(i32)
        label = recept[:, here]
        rank = jnp.where(label >= 32768, 63 - (rank >> 7), rank & 127)
        base = donor[:, here]
        plane = base >> 14
        offset = jnp.where(plane == 1, offsets[0], jnp.where(plane == 2, offsets[1], jnp.where(plane == 3, offsets[2], offsets[3])))
        chosen = high_rows == offset + (spot >> 8)
        fields = [(base >> 7) & 127, base & 127, dest[:, here], rank + 1]
        fields = [field.astype(f32) for field in fields]
        for k in range(3):
            rest = fractions[k, :, here]
            for _ in range(3):
                part = rest.astype(bf16).astype(f32)
                fields.append(part)
                rest = rest - part
        spread = jnp.concatenate([jnp.where(chosen, field, 0.0) for field in fields] + [blank], axis=0)
        spreads.append(spread.astype(bf16))
        places.append(exact(low_rows == (spot & 255)))
        held = slots == rank
        mark = [jnp.where(held, part.astype(f32), 0.0) for part in ((label + 1) >> 8, (label + 1) & 255)]
        marks.append(jnp.concatenate(mark, axis=0).astype(bf16))
        targets.append(exact(inside[:128]))

    def gathered(left, right):
        left, right = jnp.concatenate(left, axis=1), jnp.concatenate(right, axis=1)
        return lax.dot_general(left, right, NT, preferred_element_type=f32)

    both = gathered(targets, marks) * jnp.where(iota((128, 128), 1) < 64, 256.0, 1.0)
    labels[...] = both + pltpu.roll(both, 64, 1)
    total = gathered(spreads, places)

    def field(i):
        return total[i * DONOR_ROWS : (i + 1) * DONOR_ROWS]

    for i in range(4):
        table[i] = field(i)
    for i in range(3):
        table[4 + i] = field(4 + 3 * i) + field(5 + 3 * i) + field(6 + 3 * i)


def prepare(donor, fractions, dest, recept):
    numbers = jnp.concatenate([x.reshape(1, 1, -1) for x in (donor, dest, recept)], axis=0)
    return pl.pallas_call(
        prepare_kernel,
        out_shape=(
            jax.ShapeDtypeStruct((7, DONOR_ROWS, TILE), f32),
            jax.ShapeDtypeStruct((128, 128), f32),
            jax.ShapeDtypeStruct((4,), i32),
        ),
        in_specs=placed("vv"),
        out_specs=tuple(placed("vvs")),
        compiler_params=params(),
        cost_estimate=pl.CostEstimate(flops=3 * 10**9, bytes_accessed=10**6, transcendentals=0),
    )(numbers, fractions)


def pack_kernel(far, with_labels, *refs):
    if far:
        fetched, _, beyond, table, starts, given, out, source, total, state, sems = refs
        held = fetched if with_labels else fetched.at[:, 3:4]
        copies = [pltpu.make_async_copy(held.at[c], state.at[c], sems.at[c]) for c in range(4)]
    else:
        fetched, table, starts, total, source, state, sems = refs
        copies = [pltpu.make_async_copy(fetched.at[c], state.at[c], sems.at[c]) for c in range(4)]
    for copy in copies:
        copy.start()
    inner = lax.axis_index("blk") < lax.axis_size("blk") - 1
    planes = state.shape[1]
    for c in range(4):
        copies[c].wait()
        rows = slice(c * 128, c * 128 + 128)
        for x in range(planes + far):
            high, low = two_parts(state[c, x] if x < planes else jnp.where(inner, beyond[c], 0.0))
            source[0, rows, x * 128 : x * 128 + 128] = high
            source[1, rows, x * 128 : x * 128 + 128] = low
    total[...] = given[...] if far and not with_labels else jnp.zeros_like(total)
    cells = iota((128, TILE), 0)
    slots = iota((64, TILE), 0)
    first = starts[2] if far and not with_labels else 0
    last = starts[3] if far else starts[2]
    group = WHOLE_GROUP if with_labels else FAR_GROUP if far else NEAR_GROUP
    inside = 3 if with_labels else 0 if far else 2

    def interpolated(t):
        line, point, target, rank, fx, fy, fz = (table[i, pl.ds(t, 1), :] for i in range(7))
        line, point, target, rank = (v.astype(i32) for v in (line, point, target, rank))
        wy = jnp.where(cells == line, 1.0 - fy, jnp.where(cells == line + 1, fy, 0.0))
        wz = jnp.where(cells == point, 1.0 - fz, jnp.where(cells == point + 1, fz, 0.0))
        lower, upper = two_parts(wz * (1.0 - fx)), two_parts(wz * fx)
        high = [lower[0], upper[0]]
        weights = jnp.concatenate(high + high + [lower[1], upper[1]], axis=0)
        pair = sum((t >= starts[i]).astype(i32) for i in range(inside))
        both = pl.ds(pl.multiple_of(pair * 128, 128), 256) if inside else slice(0, 256)
        high, low = source[0, :, both], source[1, :, both]
        lines = jnp.dot(jnp.concatenate([high, low, high], axis=1), weights, preferred_element_type=f32)
        chosen = slots == jnp.where(t < last, rank - 1, -1)
        values = [jnp.sum(lines[c * 128 : c * 128 + 128] * wy, axis=0, keepdims=True) for c in range(4)]
        parts = []
        for which in (0, 1):
            for c in range(4):
                part = two_parts(values[c])[which].astype(f32)
                parts.append(jnp.where(chosen, part, 0.0).astype(bf16))
        return exact(cells == target), jnp.concatenate(parts, axis=0)

    def step(t, _):
        members, packed = zip(*[interpolated(first + t * group + j) for j in range(group)])
        members, packed = jnp.concatenate(members, axis=1), jnp.concatenate(packed, axis=1)
        total[...] += lax.dot_general(members, packed, NT, preferred_element_type=f32)
        return 0

    lax.fori_loop(0, (last - first + group - 1) // group, step, 0)
    if not far:
        return
    for half in range(2):
        cut = slice(half * 128, half * 128 + 128)
        low = slice(256 + half * 128, 256 + half * 128 + 128)
        out[:, 0, cut] = total[:, cut] + total[:, low]
    if with_labels:
        out[:, 0, 256:384] = given[...]


def pack_near(state, table, starts):
    return pl.pallas_call(
        functools.partial(pack_kernel, 0, False),
        out_shape=jax.ShapeDtypeStruct((128, 512), f32),
        in_specs=placed("hvs"),
        out_specs=placed("v")[0],
        scratch_shapes=[
            pltpu.VMEM((2, 512, 512), bf16),
            pltpu.VMEM(state.shape, f32),
            pltpu.SemaphoreType.DMA((4,)),
        ],
        compiler_params=params(),
        cost_estimate=pl.CostEstimate(flops=5 * 10**9, bytes_accessed=10**6, transcendentals=0),
    )(state, table, starts)


def pack_rest(first, state, below, beyond, table, starts, given):
    planes = 4 if first else 1
    return pl.pallas_call(
        functools.partial(pack_kernel, 1, first),
        out_shape=jax.ShapeDtypeStruct((128, 1, 384 if first else 256), f32),
        in_specs=placed("hhvvsv"),
        out_specs=placed("v")[0],
        scratch_shapes=[
            pltpu.VMEM((2, 512, planes * 128 + 128), bf16),
            pltpu.VMEM((128, 512), f32),
            pltpu.VMEM((4, planes, 128, 128), f32),
            pltpu.SemaphoreType.DMA((4,)),
        ],
        compiler_params=params(),
    )(state, below, beyond, table, starts, given)


def rates_of(x, state, below, beyond, metric, damping):
    row = iota((128, 128), 0)
    lane = iota((128, 128), 1)

    block = lax.axis_index("blk")
    inner = block > 0, block < lax.axis_size("blk") - 1

    def differences(c):
        here = state[c, x]
        low = jnp.where(inner[0], below[c], 0.0) if x == 0 else state[c, x - 1]
        high = jnp.where(inner[1], beyond[c], 0.0) if x == 3 else state[c, x + 1]
        up = jnp.where(row < 127, pltpu.roll(here, 127, 0), 0.0)
        down = jnp.where(row > 0, pltpu.roll(here, 1, 0), 0.0)
        right = jnp.where(lane < 127, pltpu.roll(here, 127, 1), 0.0)
        left = jnp.where(lane > 0, pltpu.roll(here, 1, 1), 0.0)
        return (high - low) * 0.5, (up - down) * 0.5, (right - left) * 0.5

    def gradient(diffs, i):
        return metric[i, x] * diffs[0] + metric[3 + i, x] * diffs[1] + metric[6 + i, x] * diffs[2]

    damp = damping[x]
    pressure = -damp * state[0, x]
    for i in range(3):
        pressure = pressure - gradient(differences(1 + i), i)
    diffs = differences(0)
    return [pressure] + [-gradient(diffs, i) - damp * state[1 + i, x] for i in range(3)]


def deposit_kernel(first, *refs):
    fetches = 5 if first else 6
    arrived, fetched, refs = refs[0], refs[1 : fetches + 1], refs[fetches + 1 :]
    if first:
        low_plane, high_plane, out, counts, cells, bounds, *scratch = refs
    else:
        counts, cells, bounds, out, *scratch = refs
    slots, total, count, sems, *held = scratch
    now, below, beyond, metric, damping = held[:5]
    copies = [pltpu.make_async_copy(fetched[i], held[i], sems.at[i]) for i in range(fetches)]
    for copy in copies:
        copy.start()
    for j in range(2):
        turned = arrived[:, 0, j * 128 : j * 128 + 128].T
        for half in range(2):
            high, low = two_parts(turned[half * 64 : half * 64 + 64])
            slots[2 * j + half] = high.astype(f32)
            slots[4 + 2 * j + half] = low.astype(f32)
    if first:
        label = arrived[:, 0, 256:384].T[:64].astype(i32) - 1
        cells[0] = (label >> 7) & 127
        cells[1] = (label >> 14) * 128 + (label & 127)
        rank = iota((64, 128), 0)
        front = (label >= 0) & (label < 32768)
        bounds[0] = (jnp.max(jnp.where(front, rank + 1, 0).astype(f32)).astype(i32) + RANKS - 1) // RANKS
        bounds[1] = jnp.min(jnp.where(label >= 32768, rank, 64).astype(f32)).astype(i32) // RANKS
        count[...] = jnp.zeros_like(count)
    total[...] = jnp.zeros_like(total)
    lines = iota((128, 128), 0)
    points = iota((256, 128), 0)

    def add(pairs, t, _):
        high, low, ones, selectors = [], [], [], []
        for j in range(RANKS):
            row = pl.ds(t * RANKS + j, 1)
            at = lines == cells[0, row, :]

            def spread(f):
                return jnp.where(at, slots[f, row, :], 0.0).astype(bf16)

            high.append(jnp.concatenate([spread(f) for f in range(4)], axis=0))
            low.append(jnp.concatenate([spread(4 + f) for f in range(4)], axis=0))
            ones.append(exact(at))
            point = cells[1, row, :]
            selectors.append(jnp.concatenate([exact(points == point - 256 * p) for p in pairs], axis=0))
        selector = jnp.concatenate(selectors + selectors, axis=1)
        added = lax.dot_general(jnp.concatenate(high + low, axis=1), selector, NT, preferred_element_type=f32)
        for i, p in enumerate(pairs):
            total[p] += added[:, i * 256 : i * 256 + 256]
        if first:
            selector = jnp.concatenate(selectors, axis=1)
            added = lax.dot_general(jnp.concatenate(ones, axis=1), selector, NT, preferred_element_type=f32)
            for i, p in enumerate(pairs):
                count[p] += added[:, i * 256 : i * 256 + 256]
        return 0

    front, back = bounds[0], bounds[1]
    lower, upper = jnp.minimum(front, back), jnp.maximum(front, back)
    lax.fori_loop(0, lower, functools.partial(add, (0,)), 0)
    lax.fori_loop(lower, front, functools.partial(add, (0, 1)), 0)
    lax.fori_loop(upper, 64 // RANKS, functools.partial(add, (1,)), 0)
    for copy in copies:
        copy.wait()
    for x in range(4):
        lanes = slice((x % 2) * 128, (x % 2) * 128 + 128)
        if first:
            counts[x] = count[x // 2, :, lanes]
        rates = rates_of(x, now, below, beyond, metric, damping)
        for c in range(4):
            fringe = total[x // 2, c * 128 : c * 128 + 128, lanes]
            rate = rates[c] + fringe - counts[x] * now[c, x]
            if first:
                out[c, x] = now[c, x] + step_size * rate
                if x in (0, 3):
                    (low_plane if x == 0 else high_plane)[c] = out[c, x]
            else:
                out[c, x] = 0.5 * (held[5][c, x] + now[c, x]) + (0.5 * step_size) * rate


def deposit(first, arrived, *operands):
    fetched = operands[: 5 if first else 6]
    shape = fetched[0].shape
    if first:
        results = (
            jax.ShapeDtypeStruct((4, 128, 128), f32),
            jax.ShapeDtypeStruct((4, 128, 128), f32),
            jax.ShapeDtypeStruct(shape, f32),
            jax.ShapeDtypeStruct(shape[1:], f32),
            jax.ShapeDtypeStruct((2, 64, 128), i32),
            jax.ShapeDtypeStruct((2,), i32),
        )
        specs, result_specs = placed("vhhhhh"), tuple(placed("vvvvvs"))
    else:
        results, result_specs = jax.ShapeDtypeStruct(shape, f32), placed("v")[0]
        specs = placed("vhhhhhhvvs")
    return pl.pallas_call(
        functools.partial(deposit_kernel, first),
        out_shape=results,
        in_specs=specs,
        out_specs=result_specs,
        scratch_shapes=[
            pltpu.VMEM((8, 64, 128), f32),
            pltpu.VMEM((2, 512, 256), f32),
            pltpu.VMEM((2, 128, 256), f32),
            pltpu.SemaphoreType.DMA((len(fetched),)),
        ]
        + [pltpu.VMEM(operand.shape, f32) for operand in fetched],
        compiler_params=params(),
    )(arrived, *operands)


def neighbours(low_plane, high_plane):
    count = lax.axis_size("blk")
    forward = [(i, (i + 1) % count) for i in range(count)]
    backward = [((i + 1) % count, i) for i in range(count)]
    beyond = lax.ppermute(low_plane, "blk", backward)
    below = lax.ppermute(high_plane, "blk", forward)
    return below, beyond


def exchange(outgoing):
    return lax.all_to_all(outgoing, ("grid", "blk"), split_axis=0, concat_axis=0, tiled=True)


def local(state, metric, damping, donor, fractions, dest, recept):
    state, metric, damping = state[0], metric[0], damping[0]
    fractions = fractions.reshape(3, 1, -1)
    dest = dest.reshape(1, -1)
    below, beyond = neighbours(state[:, 0], state[:, 3])
    table, labels, tiles = prepare(donor, fractions, dest, recept)
    arrived = exchange(pack_rest(True, state, below, beyond, table, tiles, labels))
    low_plane, high_plane, section, *kept = deposit(True, arrived, state, below, beyond, metric, damping)
    below, beyond = neighbours(low_plane, high_plane)
    partial = pack_near(section, table, tiles)
    arrived = exchange(pack_rest(False, section, below, beyond, table, tiles, partial))
    return deposit(False, arrived, section, below, beyond, metric, damping, state, *kept)[None]


def solution(mesh):
    in_specs = (
        P("grid", None, "blk", None, None),
        P("grid", None, "blk", None, None),
        P("grid", "blk", None, None),
        P("grid", "blk"),
        P("grid", None, "blk"),
        P("grid", "blk", None),
        P("grid", "blk"),
    )
    out_specs = P("grid", None, "blk", None, None)
    return jax.shard_map(local, mesh=mesh, in_specs=in_specs, out_specs=out_specs, check_vma=False)
```
